32 devices in a mesh: dp: 16 (over z, y, core), expert: 2 (over x).
Axes of the slice: x: 2, y: 2, z: 4, core: 2. Of those that a mesh axis runs over, the one named last changes fastest.
Arguments:
- tokens: bfloat16 [2048, 2048], P(('dp', 'expert')), may hold values from -16 to 16
- cotangent: bfloat16 [2048, 2048], P(('dp', 'expert')), may hold values from -8 to 8
- route: int32 [4096], P(('dp', 'expert')), may hold values from 0 to 63, as said below
- counts: int32 [32, 2], P(('dp', 'expert')), may hold values from 32 to 64, as said below
- gate_master: float32 [2, 2048, 768], P('expert', 'dp'), may hold values from -0.125 to 0.125
- up_master: float32 [2, 2048, 768], P('expert', 'dp'), may hold values from -0.125 to 0.125
- down_master: float32 [2, 2048, 768], P('expert', 'dp'), may hold values from -0.21875 to 0.21875
- first_moment: float32 [2, 3, 2048, 768], P('expert', None, 'dp'), may hold values from -2 to 2
- second_moment: float32 [2, 3, 2048, 768], P('expert', None, 'dp'), may hold values from 0.01 to 1
Outputs:
- combined: float32 [2, 3, 2048, 768], P('expert', None, 'dp')
- new_weights: float32 [2, 3, 2048, 768], P('expert', None, 'dp')
- new_first: float32 [2, 3, 2048, 768], P('expert', None, 'dp')
- new_second: float32 [2, 3, 2048, 768], P('expert', None, 'dp')
- forward: bfloat16 [2048, 2048], P(('dp', 'expert'))
The draws below stay inside these ranges and needn't reach their ends.
Inputs may be any that keep to these rules, and one draw needn't show every extreme that they name: `route`: for each device and each expert, the 64 slots name distinct local token rows. `counts`: in every draw, for some data index and some expert, every source device of that data index sends exactly 64 live slots.
All inputs are finite; a program needn't handle non-finite values.
Results may differ from the reference program's by a relative error of at most 0.011.
The reference program's roundings to bfloat16 on the way count: a program that leaves them out, or rounds other values in their place, can miss the bound.
Values may be sent and summed in bfloat16 or wider, within the bound.
No kernel may reach another device: no remote copies, remote signals or barrier semaphores. Data moves between devices by JAX's collectives and lax.ppermute only.
A program may use at most 128 MiB of HBM per device.

```python
import math
import jax
import jax.numpy as jnp
from jax import lax

D = 2048
FF = 768
ROWS = 128
EXPERTS = 2
POOL = 64
CAP = 64
LEVELS = 4
ALL_TOKENS = 2048
N_DP = 16
N_EXPERT = 2


def feature_scales(key):
    values = jnp.exp(jax.random.uniform(key, (D,), jnp.float32, jnp.log(0.5), jnp.log(5.0)))
    return values / jnp.sqrt(jnp.mean(values * values))


def draw_tokens(key, part):
    total_rows = POOL * N_DP * N_EXPERT
    scales = feature_scales(jax.random.fold_in(key, 11))
    common = jax.random.normal(jax.random.fold_in(key, 12), (D,), jnp.float32)
    noise = jax.random.normal(jax.random.fold_in(key, 15), (total_rows, D), jnp.float32)
    values = (0.7 * common[None, :] + noise) * scales[None, :]
    return jnp.clip(values, -16.0, 16.0).astype(jnp.bfloat16)


def draw_cotangent(key, part):
    total_rows = POOL * N_DP * N_EXPERT
    scales = feature_scales(jax.random.fold_in(key, 31))
    common = jax.random.normal(jax.random.fold_in(key, 32), (D,), jnp.float32)
    data_pos = (jnp.arange(total_rows, dtype=jnp.int32) // (POOL * N_EXPERT)).astype(jnp.float32)
    fraction = data_pos / max(N_DP - 1, 1)
    noise = jax.random.normal(jax.random.fold_in(key, 34), (total_rows, D), jnp.float32)
    rising = jnp.exp(fraction * jnp.log(3.0))
    values = (0.5 * common[None, :] + noise) * scales[None, :] * rising[:, None]
    values = values / jnp.sqrt(ROWS * 1.0)
    return jnp.clip(values, -8.0, 8.0).astype(jnp.bfloat16)


def draw_route(key, part):
    blocks = N_DP * N_EXPERT * N_EXPERT
    block_keys = jax.random.split(jax.random.fold_in(key, 41), blocks)
    chosen = jax.vmap(lambda block_key: jax.random.permutation(block_key, POOL)[:CAP])(block_keys)
    return chosen.reshape(-1).astype(jnp.int32)


def draw_counts(key, part):
    sources = N_DP * N_EXPERT
    base = jax.random.randint(jax.random.fold_in(key, 51), (sources, N_EXPERT), CAP // 2, CAP + 1)
    full_group = jax.random.randint(jax.random.fold_in(key, 52), (), 0, N_DP)
    full_target = jax.random.randint(jax.random.fold_in(key, 53), (), 0, N_EXPERT)
    low_source = jax.random.randint(jax.random.fold_in(key, 54), (), 0, sources)
    source_ids = jnp.arange(sources, dtype=jnp.int32)[:, None]
    target_ids = jnp.arange(N_EXPERT, dtype=jnp.int32)[None, :]
    base = jnp.where((source_ids == low_source) & (target_ids == (full_target + 1) % N_EXPERT), CAP // 2, base)
    base = jnp.where((source_ids // N_EXPERT == full_group) & (target_ids == full_target), CAP, base)
    return base.astype(jnp.int32)


def block_levels(key, extent, shards, smallest, top_value):
    loudness = 1.0
    for dim, parts in shards:
        heights = jax.random.uniform(jax.random.fold_in(jax.random.fold_in(key, 6), dim), (parts,), jnp.float32, smallest / len(shards), top_value / len(shards))
        loudness = loudness * jnp.repeat(jnp.exp(heights), extent[dim] // parts).reshape((-1,) + (1,) * (len(extent) - 1 - dim))
    return loudness


def centred(key, dims, deviation, reach, shards=(), kind=jnp.bfloat16):
    drawn = jax.random.normal(key, dims, jnp.float32) * deviation
    if len(shards) > 0:
        drawn = block_levels(key, dims, shards, -0.22, 0.18) * drawn
    return jnp.clip(drawn, min=-reach, max=reach).astype(kind)


def setup_inputs(seed: int = 0) -> dict:
    splits = jax.random.split(jax.random.key(seed), 10)
    tokens = draw_tokens(jax.random.fold_in(splits[9], 71), 0)
    cotangent = draw_cotangent(jax.random.fold_in(splits[9], 71), 0)
    route = draw_route(jax.random.fold_in(splits[9], 71), 0)
    counts = draw_counts(jax.random.fold_in(splits[9], 71), 0)
    gate_master = centred(splits[4], (EXPERTS, D, FF), D ** -0.5, 0.125, ((0, 2), (1, 16)), jnp.float32)
    up_master = centred(splits[5], (EXPERTS, D, FF), D ** -0.5, 0.125, ((0, 2), (1, 16)), jnp.float32)
    down_master = centred(splits[6], (EXPERTS, D, FF), FF ** -0.5, 0.21875, ((0, 2), (1, 16)), jnp.float32)
    first_moment = centred(splits[7], (EXPERTS, 3, D, FF), 0.3, 2.0, ((0, 2), (2, 16)), jnp.float32)
    second_moment = jnp.clip(jnp.exp(math.log(1.0) - 4.6051702 * jax.random.uniform(splits[8], (EXPERTS, 3, D, FF), jnp.float32) ** block_levels(splits[8], (EXPERTS, 3, D, FF), ((0, 2), (2, 16)), -0.2, 0.2)), 0.01, 1.0)
    return {"tokens": tokens, "cotangent": cotangent, "route": route, "counts": counts, "gate_master": gate_master, "up_master": up_master, "down_master": down_master, "first_moment": first_moment, "second_moment": second_moment}


first_decay = 0.9
second_decay = 0.95
learn_rate = 0.01
adam_eps = 1e-08
weight_decay = 0.1
adam_count = 100.0
norm_eps = 1e-06

def rounded(values):
    return lax.optimization_barrier(values.astype(jnp.bfloat16)).astype(jnp.float32)

def adasum_tree(vectors):
    for level_index in range(LEVELS):
        paired = vectors.reshape((vectors.shape[0] // 2, 2) + vectors.shape[1:])
        lower = rounded(paired[:, 0])
        upper = rounded(paired[:, 1])
        cross = lax.optimization_barrier(jnp.sum(lower * upper, axis=(2, 3)))
        lower_square = lax.optimization_barrier(jnp.sum(lower * lower, axis=(2, 3)))
        upper_square = lax.optimization_barrier(jnp.sum(upper * upper, axis=(2, 3)))
        lower_coef = 1.0 - cross / (2.0 * (lower_square + norm_eps))
        upper_coef = 1.0 - cross / (2.0 * (upper_square + norm_eps))
        vectors = lower_coef[:, :, None, None] * lower + upper_coef[:, :, None, None] * upper
    return vectors[0]

def reference(tokens, cotangent, route, counts, gate_master, up_master, down_master, first_moment, second_moment):
    capacity = ROWS // N_EXPERT
    pooled = tokens.reshape(N_DP, N_EXPERT, POOL, D)
    pooled_grads = cotangent.reshape(N_DP, N_EXPERT, POOL, D)
    routes = route.reshape(N_DP, N_EXPERT, N_EXPERT, capacity)
    limits = counts.reshape(N_DP, N_EXPERT, N_EXPERT)
    live_slots = jnp.arange(capacity, dtype=jnp.int32)[None, None, None, :] < limits[..., None]
    data_ids = jnp.arange(N_DP, dtype=jnp.int32)[:, None, None]
    source_ids = jnp.arange(N_EXPERT, dtype=jnp.int32)[None, :, None]
    forward = jnp.zeros((N_DP, N_EXPERT, POOL, D), jnp.float32)
    combined_all = []
    weights_all = []
    first_all = []
    second_all = []
    for expert_index in range(N_EXPERT):
        slot_rows = routes[:, :, expert_index, :]
        slot_live = live_slots[:, :, expert_index, :]
        token_in = jnp.where(slot_live[..., None], pooled[data_ids, source_ids, slot_rows], 0).reshape(N_DP, ROWS, D)
        grad_in = jnp.where(slot_live[..., None], pooled_grads[data_ids, source_ids, slot_rows], 0).reshape(N_DP, ROWS, D)
        w_gate = gate_master[expert_index].astype(jnp.bfloat16)
        w_up = up_master[expert_index].astype(jnp.bfloat16)
        w_down = down_master[expert_index].astype(jnp.bfloat16)

        def local_pass(pair):
            token_rows, grad_rows = pair
            gate_pre = jnp.dot(token_rows, w_gate, preferred_element_type=jnp.float32)
            up_pre = jnp.dot(token_rows, w_up, preferred_element_type=jnp.float32)
            back_hidden = jnp.dot(grad_rows, w_down, preferred_element_type=jnp.float32)
            sigmoid_gate = jax.nn.sigmoid(gate_pre)
            active_gate = gate_pre * sigmoid_gate
            hidden_act = (active_gate * up_pre).astype(jnp.bfloat16)
            d_gate = (back_hidden * up_pre * sigmoid_gate * (1.0 + gate_pre * (1.0 - sigmoid_gate))).astype(jnp.bfloat16)
            d_up = (back_hidden * active_gate).astype(jnp.bfloat16)
            grads = jnp.stack([jnp.dot(token_rows.T, d_gate, preferred_element_type=jnp.float32), jnp.dot(token_rows.T, d_up, preferred_element_type=jnp.float32), jnp.dot(grad_rows.T, hidden_act, preferred_element_type=jnp.float32)])
            return (grads, hidden_act)
        grads_all, hidden_all = lax.map(local_pass, (token_in, grad_in))
        combined = adasum_tree(grads_all)
        masters = jnp.stack([gate_master[expert_index], up_master[expert_index], down_master[expert_index]])
        new_first = first_decay * first_moment[expert_index] + (1.0 - first_decay) * combined
        new_second = second_decay * second_moment[expert_index] + (1.0 - second_decay) * combined * combined
        first_hat = new_first / (1.0 - first_decay ** adam_count)
        second_hat = new_second / (1.0 - second_decay ** adam_count)
        new_masters = masters - learn_rate * (first_hat / (jnp.sqrt(second_hat) + adam_eps) + weight_decay * masters)
        new_down = new_masters[2].astype(jnp.bfloat16)

        def project(hidden_act):
            return jnp.dot(hidden_act, new_down.T, preferred_element_type=jnp.float32).astype(jnp.bfloat16)
        outputs = lax.map(project, hidden_all).reshape(N_DP, N_EXPERT, capacity, D)
        updates = jnp.where(slot_live[..., None], outputs.astype(jnp.float32), 0.0)
        forward = forward.at[data_ids, source_ids, slot_rows].add(updates)
        combined_all.append(combined)
        weights_all.append(new_masters)
        first_all.append(new_first)
        second_all.append(new_second)
    forward_out = forward.reshape(ALL_TOKENS, D).astype(jnp.bfloat16)
    return (jnp.stack(combined_all), jnp.stack(weights_all), jnp.stack(first_all), jnp.stack(second_all), forward_out)
```

```python
import functools

import jax
import jax.numpy as jnp
from jax import lax
from jax.experimental import pallas as pl
from jax.experimental.pallas import tpu as pltpu
from jax.sharding import PartitionSpec as P

first_decay = 0.9
second_decay = 0.95
learn_rate = 0.01
adam_eps = 1e-08
weight_decay = 0.1
adam_count = 100.0
norm_eps = 1e-06
gathered_limit = 16
mask_lanes = 128
vmem_bytes = 56 * 1024 * 1024
f32 = jnp.float32
bf16 = jnp.bfloat16
any_space = pl.BlockSpec(memory_space=pl.ANY)
smem_space = pl.BlockSpec(memory_space=pltpu.SMEM)
vmem_space = pl.BlockSpec(memory_space=pltpu.VMEM)
params = pltpu.CompilerParams(vmem_limit_bytes=vmem_bytes)


def swapped(array, axis, bit):
    return lax.ppermute(array, axis, [(i, i ^ 1 << bit) for i in range(lax.axis_size(axis))])


def bits_of(size):
    return size.bit_length() - 1


def cube_gather(array, steps):
    pieces = {(0, 0): array}
    for axis, bit in steps:
        for (e, k), piece in list(pieces.items()):
            key = (e ^ (1 << bit), k) if axis == "expert" else (e, k ^ (1 << bit))
            pieces[key] = swapped(piece, axis, bit)
    return pieces


def tree_sum(value, bits):
    for bit in range(bits):
        value = value + swapped(value, "dp", bit)
    return value


def nt(a, b):
    return lax.dot_general(a, b, (((1,), (1,)), ((), ())), preferred_element_type=f32)


def tn(a, b):
    return lax.dot_general(a, b, (((0,), (0,)), ((), ())), preferred_element_type=f32)


def tree_weights(entry, count):
    gram = {(i, j): entry(i, j) for i in range(count) for j in range(i, count)}
    weights = [None] * count
    size = count
    while size > 1:
        scale = []
        for j in range(0, size, 2):
            cross = gram[j, j + 1]
            scale.append(1.0 - cross / (2.0 * (gram[j, j] + norm_eps)))
            scale.append(1.0 - cross / (2.0 * (gram[j + 1, j + 1] + norm_eps)))
        span = count // size
        for leaf in range(count):
            factor = scale[leaf // span]
            weights[leaf] = factor if weights[leaf] is None else weights[leaf] * factor
        full = lambda i, j: gram[min(i, j), max(i, j)] * (scale[i] * scale[j])
        size //= 2
        if size > 1:
            gram = {
                (i, j): full(2 * i, 2 * j)
                + full(2 * i, 2 * j + 1)
                + full(2 * i + 1, 2 * j)
                + full(2 * i + 1, 2 * j + 1)
                for i in range(size)
                for j in range(i, size)
            }
    return weights


def prepare_kernel(route_ref, counts_ref, cot_ref, gate_ref, up_ref, down_ref, sent_ref, ext_ref):
    group, mats = sent_ref.shape[0], 3
    part = sent_ref.shape[1] // mats
    pool, width = cot_ref.shape
    experts, capacity = route_ref.shape
    for index, ref in enumerate((gate_ref, up_ref, down_ref)):
        turned = ref[...].T.astype(bf16)
        for k in range(group):
            sent_ref[k, index * part : (index + 1) * part, :] = turned[k * part : (k + 1) * part, :]
    ext_ref[:, :width] = cot_ref[...]
    ids = lax.broadcasted_iota(jnp.int32, (pool, capacity), 0)
    slots = lax.broadcasted_iota(jnp.int32, (pool, capacity), 1)
    lanes = lax.broadcasted_iota(jnp.int32, (pool, mask_lanes), 1)
    flags = jnp.zeros((pool, mask_lanes), f32)
    for e in range(experts):
        named = (ids == route_ref[e : e + 1, :]) & (slots < counts_ref[0, e])
        found = jnp.sum(named.astype(f32), axis=1, keepdims=True)
        flags = jnp.where(lanes == e, found, flags)
    ext_ref[:, width:] = flags.astype(bf16)


def gather_kernel(group, experts, idx_ref, *refs):
    count = group * experts
    tok, cot = refs[:count], refs[count : 2 * count]
    held = refs[2 * count : -11]
    hid_ref, dgate_ref, dup_ref, gram_ref, x_out, y_out = refs[-11:-5]
    x_ref, y_ref, w_ref, sems, out_sems = refs[-5:]
    slot, expert, outer_index = idx_ref[0], idx_ref[1], idx_ref[2]
    pool = tok[0].shape[0]
    rows = experts * pool
    part, total = hid_ref.shape
    width = x_ref.shape[1]
    loads = []
    for which, (pieces, into) in enumerate(((tok, x_ref), (cot, y_ref))):
        made = []
        for e in range(experts):
            for k in range(group):
                n = e * group + k
                at = ((slot ^ k) * experts + (expert ^ e)) * pool
                made.append(
                    pltpu.make_async_copy(
                        pieces[n], into.at[pl.ds(pl.multiple_of(at, pool), pool), :], sems.at[which, n]
                    )
                )
        for copy in made:
            copy.start()
        loads.append(made)
    per = held[0].shape[0]
    outer = per * len(held)
    block_rows = held[0].shape[3]
    for o in range(outer):
        for h, ref in enumerate(held):
            @pl.when(((outer_index ^ o) // per) == h)
            def _(ref=ref, o=o):
                source = ref.at[(outer_index ^ o) % per]
                for b in range(group):
                    at = (o * group + b) * block_rows
                    w_ref[:, at : at + block_rows] = source[b]
    for copy in loads[0]:
        copy.wait()
    x_save = pltpu.make_async_copy(x_ref, x_out, out_sems.at[0])
    x_save.start()
    pre = nt(w_ref[: 2 * part, :], x_ref[...])
    for copy in loads[1]:
        copy.wait()
    y_save = pltpu.make_async_copy(y_ref, y_out, out_sems.at[1])
    y_save.start()
    back_hidden = nt(w_ref[2 * part :, :], y_ref[:, :width])
    pick = lax.broadcasted_iota(jnp.int32, (8, mask_lanes), 1) == expert
    mask = nt(pick.astype(bf16), y_ref[:, width:])[0:1] > 0.5
    gate_pre, up_pre = pre[:part], pre[part:]
    sigmoid_gate = jax.nn.sigmoid(gate_pre)
    active_gate = gate_pre * sigmoid_gate
    kept = lambda value: jnp.where(mask, value, 0.0).astype(bf16)
    hid_ref[...] = kept(active_gate * up_pre)
    dgate_ref[...] = kept(
        back_hidden * up_pre * sigmoid_gate * (1.0 + gate_pre * (1.0 - sigmoid_gate))
    )
    dup_ref[...] = kept(back_hidden * active_gate)
    shape = gram_ref.shape
    row_ids = lax.broadcasted_iota(jnp.int32, shape, 0)
    lane_ids = lax.broadcasted_iota(jnp.int32, shape, 1)
    gram = jnp.zeros(shape, f32)
    for a in range(group):
        low = a * rows
        mine = slice(low, low + rows)
        outer_x = nt(x_ref[mine, :], x_ref[low:, :])
        outer_y = nt(y_ref[mine, :width], y_ref[low:, :width])
        for m, (ref, prod) in enumerate(
            ((dgate_ref, outer_x), (dup_ref, outer_x), (hid_ref, outer_y))
        ):
            both = prod * tn(ref[:, mine], ref[:, low:])
            for b in range(a, group):
                value = jnp.sum(both[:, (b - a) * rows : (b - a + 1) * rows], keepdims=True)
                gram = jnp.where((row_ids == m * group + a) & (lane_ids == b), value, gram)
    gram_ref[...] = gram
    x_save.wait()
    y_save.wait()


def vector_kernel(group, mats, gram_ref, in_ref, *refs):
    factors, out_ref = refs[:-1], refs[-1]
    part, total = factors[0].shape
    rows = total // group
    count, _, block_rows = out_ref.shape
    width = count * block_rows
    scaled = []
    for m, ref in zip(mats, factors):
        entry = lambda i, j: jnp.full((1, rows), gram_ref[m * group + i, j], f32)
        weights = tree_weights(entry, group)
        scaled.append(
            jnp.concatenate(
                [
                    (ref[:, d * rows : (d + 1) * rows].astype(f32) * weights[d]).astype(bf16)
                    for d in range(group)
                ],
                axis=1,
            )
        )
    left = jnp.concatenate(scaled, axis=0)
    vector = jnp.dot(left, in_ref[:, :width], preferred_element_type=f32).astype(bf16)
    for i in range(count):
        out_ref[i] = vector[:, i * block_rows : (i + 1) * block_rows]


def call(kernel, outs, args, in_specs, scratch=(), out_specs=None, aliases=None, name=None):
    return pl.pallas_call(
        kernel,
        out_shape=outs,
        in_specs=in_specs,
        out_specs=out_specs if out_specs is not None else jax.tree.map(lambda _: vmem_space, outs),
        scratch_shapes=list(scratch),
        compiler_params=params,
        input_output_aliases=aliases or {},
        name=name,
    )(*args)


def coefficients(gram):
    mats, count = gram.shape[0], gram.shape[1]
    weights = jnp.ones((mats, count), f32)
    while gram.shape[1] > 1:
        pairs = gram.shape[1] // 2
        blocks = gram.reshape(mats, pairs, 2, pairs, 2)
        diag = jnp.stack([blocks[:, j, :, j, :] for j in range(pairs)], axis=1)
        cross = diag[:, :, 0, 1]
        lower = 1.0 - cross / (2.0 * (diag[:, :, 0, 0] + norm_eps))
        upper = 1.0 - cross / (2.0 * (diag[:, :, 1, 1] + norm_eps))
        scale = jnp.stack([lower, upper], axis=2).reshape(mats, 2 * pairs)
        weights = weights * jnp.repeat(scale, count // (2 * pairs), axis=1)
        gram = gram * scale[:, :, None] * scale[:, None, :]
        gram = gram.reshape(mats, pairs, 2, pairs, 2).sum((2, 4))
    return weights


def shards(
    tokens,
    cotangent,
    route,
    counts,
    gate_master,
    up_master,
    down_master,
    first_moment,
    second_moment,
):
    experts = lax.axis_size("expert")
    dp = lax.axis_size("dp")
    group = max(1, min(gathered_limit // experts, dp))
    inner_bits = bits_of(group)
    outer_bits = bits_of(dp // group)
    outer = dp // group
    pool, width = tokens.shape
    rows = experts * pool
    block_rows, hidden_width = gate_master.shape[1:]
    part = hidden_width // group
    my_dp = lax.axis_index("dp")
    slot_index = my_dp % group
    outer_index = my_dp // group
    expert_index = lax.axis_index("expert")
    groups = [[o * group + s for s in range(group)] for o in range(outer)]
    capacity = route.shape[0] // experts

    my_ids = jnp.stack([slot_index, expert_index, outer_index]).astype(jnp.int32)
    sds = jax.ShapeDtypeStruct
    sent, grads_ext = call(
        prepare_kernel,
        (sds((group, 3 * part, block_rows), bf16), sds((pool, width + mask_lanes), bf16)),
        (route.reshape(experts, capacity), counts, cotangent, gate_master[0], up_master[0], down_master[0]),
        [vmem_space, smem_space] + [vmem_space] * 4,
        name="prepare",
    )
    own_group = lax.all_to_all(sent, "dp", 0, 0, axis_index_groups=groups, tiled=True)
    held = [own_group[None]]
    for bit in range(outer_bits):
        held = [jnp.concatenate(held)] if len(held) > 1 else held
        held = [held[0], swapped(held[0], "dp", inner_bits + bit)]
    dp_steps = [("dp", b) for b in reversed(range(inner_bits))]
    ex_steps = [("expert", b) for b in range(bits_of(experts))]
    core_step = dp_steps[-1:]
    steps_t = dp_steps[:-1] + ex_steps + core_step
    steps_c = dp_steps[:-1][:1] + ex_steps + dp_steps[:-1][1:] + core_step
    keys = [(e, k) for e in range(experts) for k in range(group)]
    token_pieces = cube_gather(tokens, steps_t)
    grad_pieces = cube_gather(grads_ext, steps_c)
    total = group * rows
    factor = sds((part, total), bf16)
    hidden, d_gate, d_up, gram, token_all, grad_all = call(
        functools.partial(gather_kernel, group, experts),
        (
            factor,
            factor,
            factor,
            sds((-(-3 * group // 8) * 8, 128), f32),
            sds((total, width), bf16),
            sds((total, width + mask_lanes), bf16),
        ),
        (my_ids, *[token_pieces[k] for k in keys], *[grad_pieces[k] for k in keys], *held),
        [smem_space] + [any_space] * (2 * len(keys)) + [vmem_space] * len(held),
        scratch=(
            pltpu.VMEM((total, width), bf16),
            pltpu.VMEM((total, width + mask_lanes), bf16),
            pltpu.VMEM((3 * part, width), bf16),
            pltpu.SemaphoreType.DMA((2, len(keys))),
            pltpu.SemaphoreType.DMA((2,)),
        ),
        out_specs=(vmem_space,) * 4 + (any_space,) * 2,
        name="forward_and_gram",
    )
    gram = tree_sum(gram, inner_bits)

    def local_tree(left, mats, factors):
        vector = call(
            functools.partial(vector_kernel, group, mats),
            sds((dp, len(mats) * part, block_rows), bf16),
            (gram, left, *factors),
            [smem_space] + [vmem_space] * (1 + len(factors)),
            name="local_tree",
        )
        got = lax.all_to_all(vector, "dp", 0, 0, tiled=True)
        got = got.reshape(outer, group, len(mats), part, block_rows).transpose(2, 0, 1, 3, 4)
        got = got.reshape(len(mats), outer, hidden_width, block_rows).astype(f32)
        if outer > 2:
            last = jnp.einsum("miab,mjab->mij", got, got, precision=lax.Precision.HIGHEST)
        else:
            last = (got[:, :, None] * got[:, None]).sum((3, 4))
        coef = coefficients(tree_sum(last, inner_bits + outer_bits))
        total = (coef[:, :, None, None] * got).sum(1)
        return total.transpose(0, 2, 1)

    masters = jnp.stack([gate_master[0], up_master[0], down_master[0]])
    down_sum = local_tree(grad_all, (2,), [hidden])
    pair_sum = local_tree(token_all, (0, 1), [d_gate, d_up])

    def adam(total, pick):
        first = first_decay * first_moment[0, pick] + (1.0 - first_decay) * total
        second = second_decay * second_moment[0, pick] + (1.0 - second_decay) * total * total
        first_hat = first / (1.0 - first_decay**adam_count)
        second_hat = second / (1.0 - second_decay**adam_count)
        old = masters[pick]
        new = old - learn_rate * (first_hat / (jnp.sqrt(second_hat) + adam_eps) + weight_decay * old)
        return total, new, first, second

    down_out = adam(down_sum, slice(2, 3))
    pair_out = adam(pair_sum, slice(0, 2))
    combined, new_masters, new_first, new_second = (
        jnp.concatenate([a, b])[None] for a, b in zip(pair_out, down_out)
    )

    new_down = down_out[1][0].astype(bf16)[None]
    for bit in range(outer_bits):
        other = swapped(new_down, "dp", inner_bits + bit)
        is_lower = (outer_index >> bit) & 1 == 0
        new_down = jnp.concatenate(
            [jnp.where(is_lower, new_down, other), jnp.where(is_lower, other, new_down)]
        )
    new_down = new_down.reshape(outer * block_rows, hidden_width)
    hidden_all = lax.all_gather(hidden, "dp", axis=0, axis_index_groups=groups, tiled=True)
    slot_outputs = lax.dot_general(
        hidden_all, new_down, (((0,), (1,)), ((), ())), preferred_element_type=f32
    ).astype(bf16)
    slot_outputs = slot_outputs.reshape(group, experts, pool, outer * block_rows)
    returned = lax.all_to_all(slot_outputs, "expert", 1, 1, tiled=True)
    summed = returned.astype(f32).sum(1).astype(bf16)
    columns = lax.all_to_all(summed, "dp", 0, 0, axis_index_groups=groups, tiled=True)
    columns = columns.reshape(group, pool, outer, block_rows).transpose(1, 2, 0, 3)
    forward = columns.reshape(pool, width)
    return (combined, new_masters, new_first, new_second, forward)


def solution(mesh):
    in_specs = (
        P(("dp", "expert"), None),
        P(("dp", "expert"), None),
        P(("dp", "expert")),
        P(("dp", "expert"), None),
        P("expert", "dp", None),
        P("expert", "dp", None),
        P("expert", "dp", None),
        P("expert", None, "dp", None),
        P("expert", None, "dp", None),
    )
    out_specs = (
        P("expert", None, "dp", None),
        P("expert", None, "dp", None),
        P("expert", None, "dp", None),
        P("expert", None, "dp", None),
        P(("dp", "expert"), None),
    )
    return jax.shard_map(shards, mesh=mesh, in_specs=in_specs, out_specs=out_specs, check_vma=False)
```

```python
import functools

import jax
import jax.numpy as jnp
from jax import lax
from jax.experimental import pallas as pl
from jax.experimental.pallas import tpu as pltpu
from jax.sharding import PartitionSpec as P

first_decay = 0.9
second_decay = 0.95
learn_rate = 0.01
adam_eps = 1e-08
weight_decay = 0.1
adam_count = 100.0
norm_eps = 1e-06
gathered_limit = 16
mask_lanes = 128
mebi = 1024 * 1024
vmem_bytes = 14 * mebi
vmem_most = 56 * mebi
f32 = jnp.float32
bf16 = jnp.bfloat16
any_space = pl.BlockSpec(memory_space=pl.ANY)
smem_space = pl.BlockSpec(memory_space=pltpu.SMEM)
vmem_space = pl.BlockSpec(memory_space=pltpu.VMEM)


def swapped(array, axis, bit):
    return lax.ppermute(array, axis, [(i, i ^ 1 << bit) for i in range(lax.axis_size(axis))])


def bits_of(size):
    return size.bit_length() - 1


def cube_gather(array, steps):
    pieces = {(0, 0): array}
    for axis, bit in steps:
        for (e, k), piece in list(pieces.items()):
            key = (e ^ (1 << bit), k) if axis == "expert" else (e, k ^ (1 << bit))
            pieces[key] = swapped(piece, axis, bit)
    return pieces


def waved_gather(mine, x_rows, sent, exchange, ids):
    z = lambda value: swapped(value, "dp", 2)
    y = lambda value: swapped(value, "dp", 1)
    x = lambda value: swapped(value, "expert", 0)
    from_z, from_y, from_x = z(mine), y(mine), x(mine)
    weights = exchange(sent)
    from_z, from_y, from_x, weights = lax.optimization_barrier((from_z, from_y, from_x, weights))
    from_zy, from_zx = y(from_z), x(from_z)
    from_yx = [x(from_y[:x_rows]), y(from_x[x_rows:])]
    from_zyx = [x(from_zy[:x_rows]), y(from_zx[x_rows:])]
    from_z, from_y, from_x, mine, ids, *_ = lax.optimization_barrier(
        (from_z, from_y, from_x, mine, ids, from_zy, from_zx)
    )
    pieces = {
        (0, 0): [mine],
        (0, 4): [from_z],
        (0, 2): [from_y],
        (1, 0): [from_x],
        (0, 6): [from_zy],
        (1, 4): [from_zx],
        (1, 2): from_yx,
        (1, 6): from_zyx,
    }
    for (e, k), held in list(pieces.items()):
        pieces[e, k | 1] = [swapped(piece, "dp", 0) for piece in held]
    return pieces, weights, ids


def tree_sum(value, bits, first=0):
    for bit in range(first, bits):
        value = value + swapped(value, "dp", bit)
    return value


def nt(a, b):
    return lax.dot_general(a, b, (((1,), (1,)), ((), ())), preferred_element_type=f32)


def tn(a, b):
    return lax.dot_general(a, b, (((0,), (0,)), ((), ())), preferred_element_type=f32)


def tree_weights(entry, count):
    gram = {(i, j): entry(i, j) for i in range(count) for j in range(i, count)}
    weights = [None] * count
    size = count
    while size > 1:
        scale = []
        for j in range(0, size, 2):
            cross = gram[j, j + 1]
            scale.append(1.0 - cross / (2.0 * (gram[j, j] + norm_eps)))
            scale.append(1.0 - cross / (2.0 * (gram[j + 1, j + 1] + norm_eps)))
        span = count // size
        for leaf in range(count):
            factor = scale[leaf // span]
            weights[leaf] = factor if weights[leaf] is None else weights[leaf] * factor
        full = lambda i, j: gram[min(i, j), max(i, j)] * (scale[i] * scale[j])
        size //= 2
        if size > 1:
            gram = {
                (i, j): full(2 * i, 2 * j)
                + full(2 * i, 2 * j + 1)
                + full(2 * i + 1, 2 * j)
                + full(2 * i + 1, 2 * j + 1)
                for i in range(size)
                for j in range(i, size)
            }
    return weights


def prepare_kernel(
    route_ref, counts_ref, tok_ref, cot_ref, gate_ref, up_ref, down_ref, out_ref, sent_ref
):
    group, part = sent_ref.shape[0], sent_ref.shape[1] // 3
    for index, ref in enumerate((gate_ref, up_ref, down_ref)):
        turned = ref[...].T.astype(bf16)
        for k in range(group):
            sent_ref[k, index * part : (index + 1) * part, :] = turned[k * part : (k + 1) * part, :]
    pool, width = cot_ref.shape
    experts, capacity = route_ref.shape
    out_ref[:pool, :width] = tok_ref[...]
    out_ref[:pool, width:] = jnp.zeros((pool, mask_lanes), bf16)
    out_ref[pool:, :width] = cot_ref[...]
    ids = lax.broadcasted_iota(jnp.int32, (pool, capacity), 0)
    slots = lax.broadcasted_iota(jnp.int32, (pool, capacity), 1)
    lanes = lax.broadcasted_iota(jnp.int32, (pool, mask_lanes), 1)
    flags = jnp.zeros((pool, mask_lanes), f32)
    for e in range(experts):
        named = (ids == route_ref[e : e + 1, :]) & (slots < counts_ref[0, e])
        found = jnp.sum(named.astype(f32), axis=1, keepdims=True)
        flags = jnp.where(lanes == e, found, flags)
    out_ref[pool:, width:] = flags.astype(bf16)


def place_rows(layout, refs, into, first, lanes, rows, pool, members):
    for (e, k), held in layout.items():
        low, at = 0, k * rows + e * pool
        for index, count in held:
            begin, end = max(low, first), min(low + count, first + pool)
            if begin < end and k in members:
                source = refs[index][begin - low : end - low, :lanes]
                into[at + begin - first : at + end - first, :] = source
            low += count


def gather_kernel(layout, experts, group, pool, pieces, idx_ref, *refs):
    shared, held, refs = refs[:pieces], refs[pieces:-9], refs[-9:]
    hid_ref, hid_abs_ref, dgate_ref, dup_ref, gram_ref, x_ref, y_ref, w_ref, row_ref = refs
    slot, expert, outer_index = idx_ref[0], idx_ref[1], idx_ref[2]
    part, total = hid_ref.shape
    rows = total // group
    width = x_ref.shape[1]
    per, _, _, block_rows = held[0].shape
    for o in range(per * len(held)):
        for h, ref in enumerate(held):

            @pl.when(((outer_index ^ o) // per) == h)
            def _(ref=ref, o=o):
                source = ref.at[(outer_index ^ o) % per]
                for b in range(group):
                    at = (o * group + b) * block_rows
                    w_ref[:, at : at + block_rows] = source[b]

    row_ref[...] = jnp.zeros_like(row_ref)
    pick = lax.broadcasted_iota(jnp.int32, (8, mask_lanes), 1) == expert
    both_members = max(1, min(group, 256 // rows))
    for first in range(0, group, both_members):
        members = range(first, first + both_members)
        mine, end = slice(first * rows, (first + both_members) * rows), (first + both_members) * rows
        place_rows(layout, shared, x_ref, 0, width, rows, pool, members)
        place_rows(layout, shared, y_ref, pool, width + mask_lanes, rows, pool, members)
        pre = nt(w_ref[: 2 * part, :], x_ref[mine, :])
        outer_x = nt(x_ref[mine, :], x_ref[:end, :])
        back_hidden = nt(w_ref[2 * part :, :], y_ref[mine, :width])
        outer_y = nt(y_ref[mine, :width], y_ref[:end, :width])
        mask = nt(pick.astype(bf16), y_ref[mine, width:])[0:1] > 0.5
        gate_pre, up_pre = pre[:part], pre[part:]
        sigmoid_gate = jax.nn.sigmoid(gate_pre)
        active_gate = gate_pre * sigmoid_gate
        kept = lambda value: jnp.where(mask, value, 0.0).astype(bf16)
        hidden = kept(active_gate * up_pre)
        hid_ref[:, mine] = hidden
        for n, k in enumerate(members):
            at = pl.multiple_of((slot ^ k) * rows, rows)
            hid_abs_ref[:, pl.ds(at, rows)] = hidden[:, n * rows : (n + 1) * rows]
        dgate_ref[:, mine] = kept(
            back_hidden * up_pre * sigmoid_gate * (1.0 + gate_pre * (1.0 - sigmoid_gate))
        )
        dup_ref[:, mine] = kept(back_hidden * active_gate)
        for m, (ref, prod) in enumerate(
            ((dgate_ref, outer_x), (dup_ref, outer_x), (hid_ref, outer_y))
        ):
            both = prod * tn(ref[:, mine], ref[:, :end])
            for n, k in enumerate(members):
                sums = both[n * rows : (n + 1) * rows, : (k + 1) * rows].sum(0, keepdims=True)
                row_ref[m * group + k : m * group + k + 1, : (k + 1) * rows] = sums
    lanes = lax.broadcasted_iota(jnp.int32, gram_ref.shape, 1)
    relative = jnp.zeros(gram_ref.shape, f32)
    for k in range(group):
        sums = row_ref[:, k * rows : (k + 1) * rows].sum(1, keepdims=True)
        relative = jnp.where(lanes == (slot ^ k), sums, relative)
    row_ids = lax.broadcasted_iota(jnp.int32, gram_ref.shape, 0)
    gram = jnp.zeros(gram_ref.shape, f32)
    for m in range(3):
        for k in range(group):
            row = relative[m * group + k : m * group + k + 1]
            gram = jnp.where(row_ids == m * group + (slot ^ k), row, gram)
    gram_ref[...] = gram


def vector_kernel(group, mats, idx_ref, gram_ref, in_ref, *refs):
    factors, out_ref = refs[:-1], refs[-1]
    part, total = factors[0].shape
    rows = total // group
    count, _, block_rows = out_ref.shape
    width = count * block_rows
    slot = idx_ref[0]
    scaled = []
    for m, ref in zip(mats, factors):

        def entry(i, j):
            a, b = slot ^ i, slot ^ j
            value = gram_ref[m * group + a, b]
            if i != j:
                value = value + gram_ref[m * group + b, a]
            return jnp.full((1, rows), value, f32)

        weights = tree_weights(entry, group)
        scaled.append(
            jnp.concatenate(
                [
                    (ref[:, d * rows : (d + 1) * rows].astype(f32) * weights[d]).astype(bf16)
                    for d in range(group)
                ],
                axis=1,
            )
        )
    left = jnp.concatenate(scaled, axis=0)
    vector = jnp.dot(left, in_ref[:, :width], preferred_element_type=f32).astype(bf16)
    for i in range(count):
        out_ref[i] = vector[:, i * block_rows : (i + 1) * block_rows]


def update_kernel(group, mats, gram_ref, got_ref, *refs):
    masters = refs[:mats]
    first_ref, second_ref = refs[mats : mats + 2]
    outs = refs[-5:] if mats == 1 else refs[-4:]
    sum_ref, new_ref, new_first_ref, new_second_ref = outs[:4]
    outer = got_ref.shape[0] // group
    block_rows = got_ref.shape[2]
    part = got_ref.shape[1] // mats
    for m in range(mats):
        entry = lambda i, j: jnp.full((1, block_rows), gram_ref[m * outer + i, j], f32)
        weights = tree_weights(entry, outer)
        total = 0.0
        for o in range(outer):
            held = [
                got_ref[o * group + s, m * part : (m + 1) * part, :].astype(f32)
                for s in range(group)
            ]
            total = total + weights[o] * jnp.concatenate(held, axis=0)
        total = total.T
        first = first_decay * first_ref[m] + (1.0 - first_decay) * total
        second = second_decay * second_ref[m] + (1.0 - second_decay) * total * total
        first_hat = first / (1.0 - first_decay**adam_count)
        second_hat = second / (1.0 - second_decay**adam_count)
        old = masters[m][...]
        new = old - learn_rate * (first_hat / (jnp.sqrt(second_hat) + adam_eps) + weight_decay * old)
        sum_ref[m] = total
        new_ref[m] = new
        new_first_ref[m] = first
        new_second_ref[m] = second
        if mats == 1:
            outs[-1][...] = new.astype(bf16)


def project_kernel(group, idx_ref, *refs):
    parts, downs, (out_ref, hidden_ref, all_ref) = refs[:group], refs[group:-3], refs[-3:]
    slot, expert, outer_index = idx_ref[0], idx_ref[1], idx_ref[2]
    bits, part = bits_of(group), parts[0].shape[0]
    for n, ref in enumerate(parts):
        relative = sum((n >> b & 1) << (bits - 1 - b) for b in range(bits))
        at = pl.multiple_of((slot ^ relative) * part, 16)
        hidden_ref[pl.ds(at, part), :] = ref[...]
    per, block_rows = downs[0].shape[:2]
    for o in range(per * len(downs)):
        for h, ref in enumerate(downs):

            @pl.when(((outer_index ^ o) // per) == h)
            def _(ref=ref, o=o):
                all_ref[o * block_rows : (o + 1) * block_rows, :] = ref[(outer_index ^ o) % per]

    made = lax.dot_general(
        hidden_ref[...], all_ref[...], (((0,), (1,)), ((), ())), preferred_element_type=f32
    )
    experts, pool = out_ref.shape[1], out_ref.shape[2]
    for d in range(out_ref.shape[0]):
        for e in range(experts):
            at = (d * experts + e) * pool
            out_ref[d, expert ^ e] = made[at : at + pool].astype(bf16)


def finish_kernel(experts, block_rows, got_ref, out_ref):
    group = got_ref.shape[0] // experts
    for o in range(got_ref.shape[2] // block_rows):
        for s in range(group):
            lanes = slice(o * block_rows, (o + 1) * block_rows)
            total = got_ref[s * experts, :, lanes].astype(f32)
            for e in range(1, experts):
                total = total + got_ref[s * experts + e, :, lanes].astype(f32)
            at = (o * group + s) * block_rows
            out_ref[:, at : at + block_rows] = total.astype(bf16)


def call(kernel, outs, args, in_specs, scratch=(), out_specs=None, aliases=None, name=None, grid=(), vmem=vmem_bytes):
    return pl.pallas_call(
        kernel,
        out_shape=outs,
        grid=grid,
        in_specs=in_specs,
        out_specs=out_specs if out_specs is not None else jax.tree.map(lambda _: vmem_space, outs),
        scratch_shapes=list(scratch),
        compiler_params=pltpu.CompilerParams(vmem_limit_bytes=min(vmem, vmem_most)),
        input_output_aliases=aliases or {},
        name=name,
    )(*args)


def after(value, *others):
    return lax.optimization_barrier((value, *others))[0]


def shards(
    tokens,
    cotangent,
    route,
    counts,
    gate_master,
    up_master,
    down_master,
    first_moment,
    second_moment,
):
    experts = lax.axis_size("expert")
    dp = lax.axis_size("dp")
    group = max(1, min(gathered_limit // experts, dp))
    inner_bits = bits_of(group)
    outer_bits = bits_of(dp // group)
    outer = dp // group
    dp_bits = inner_bits + outer_bits
    pool, width = tokens.shape
    rows = experts * pool
    total = group * rows
    block_rows, hidden_width = gate_master.shape[1:]
    part = hidden_width // group
    my_dp = lax.axis_index("dp")
    expert_index = lax.axis_index("expert")
    my_ids = jnp.stack([my_dp % group, expert_index, my_dp // group]).astype(jnp.int32)
    groups = [[o * group + s for s in range(group)] for o in range(outer)]
    cubes = [[o * group * experts + s for s in range(group * experts)] for o in range(outer)]
    capacity = route.shape[0] // experts
    sds = jax.ShapeDtypeStruct
    masters = [gate_master[0], up_master[0], down_master[0]]

    mine, sent = call(
        prepare_kernel,
        (
            sds((2 * pool, width + mask_lanes), bf16),
            sds((group, 3 * part, block_rows), bf16),
        ),
        (route.reshape(experts, capacity), counts, tokens, cotangent, *masters),
        [vmem_space, smem_space] + [vmem_space] * 5,
        name="prepare",
        vmem=vmem_most,
    )
    exchange = lambda sent: lax.all_to_all(
        sent, "dp", 0, 0, axis_index_groups=groups, tiled=True
    )
    if inner_bits == 3 and experts == 2:
        pieces, own_group, my_ids = waved_gather(
            mine, -(-5 * pool // 64) * 16, sent, exchange, my_ids
        )
    else:
        steps = [("expert", b) for b in range(bits_of(experts))]
        steps += [("dp", b) for b in reversed(range(inner_bits))]
        pieces = {key: [value] for key, value in cube_gather(mine, steps).items()}
        own_group = exchange(sent)
    shared, layout = [], {}
    for key, parts in pieces.items():
        layout[key] = [(len(shared) + n, piece.shape[0]) for n, piece in enumerate(parts)]
        shared += parts
    held = [own_group[None]]
    for bit in range(outer_bits):
        held = [jnp.concatenate(held)] if len(held) > 1 else held
        held = [held[0], swapped(held[0], "dp", inner_bits + bit)]
    wide = width + mask_lanes
    factor = sds((part, total), bf16)
    gram_rows = -(-3 * group // 8) * 8
    rows_bytes, weight_bytes = 4 * total * wide, 6 * part * width
    hidden, hidden_own, d_gate, d_up, gram, token_all, grad_all = call(
        functools.partial(gather_kernel, layout, experts, group, pool, len(shared)),
        (
            *(factor,) * 4,
            sds((gram_rows, 128), f32),
            sds((total, width), bf16),
            sds((total, wide), bf16),
        ),
        (my_ids, *shared, *held),
        [smem_space] + [vmem_space] * (len(shared) + len(held)),
        scratch=(
            pltpu.VMEM((3 * part, width), bf16),
            pltpu.VMEM((gram_rows, total), f32),
        ),
        name="forward_and_gram",
        vmem=5 * rows_bytes // 2 + 3 * weight_bytes + 4 * total * total * (outer // 4),
    )
    gram = tree_sum(gram, inner_bits)

    def local_vector(left, mats, factors):
        return call(
            functools.partial(vector_kernel, group, mats),
            sds((dp, len(mats) * part, block_rows), bf16),
            (my_ids, gram, left, *factors),
            [smem_space] * 2 + [vmem_space] * (1 + len(factors)),
            vmem=rows_bytes + 3 * len(mats) * 4 * part * width + 4 * mebi,
            name="local_tree",
        )

    def last_gram(got, mats):
        wide = got.reshape(outer, group, mats, part, block_rows).transpose(2, 0, 1, 3, 4)
        wide = wide.reshape(mats, outer, hidden_width, block_rows).astype(f32)
        if outer > 2:
            products = jnp.einsum("miab,mjab->mij", wide, wide, precision=lax.Precision.HIGHEST)
        else:
            products = (wide[:, :, None] * wide[:, None]).sum((3, 4))
        return tree_sum(products.reshape(mats * outer, outer), half)

    def update(got, products, mats, start, olds, previous):
        block = pl.BlockSpec((mats, block_rows, hidden_width), lambda i: (start, 0, 0))
        whole = sds((3, block_rows, hidden_width), f32)
        kernel = functools.partial(update_kernel, group, mats)
        outs, out_specs = (whole,) * 4, (block,) * 4
        if mats == 1:
            outs += (sds((block_rows, hidden_width), bf16),)
            out_specs += (vmem_space,)
        return call(
            kernel,
            outs,
            (products, got, *olds, first_moment[0], second_moment[0], *previous),
            [smem_space] + [vmem_space] * (1 + mats) + [block] * 2 + [any_space] * len(previous),
            out_specs=out_specs,
            aliases={4 + mats + i: i for i in range(len(previous))},
            grid=(1,),
            name="update",
            vmem=4 * got.shape[0] * got.shape[1] * 256 + 10 * mebi,
        )

    down_vector = local_vector(grad_all, (2,), [hidden])
    pair_vector = local_vector(token_all, (0, 1), [d_gate, d_up])
    exchange_rows = lambda vector: lax.all_to_all(vector, "dp", 0, 0, tiled=True)
    down_got = exchange_rows(after(down_vector, pair_vector))
    hidden_parts = [after(hidden_own, pair_vector)]
    for bit in reversed(range(inner_bits)):
        hidden_parts += [swapped(piece, "dp", bit) for piece in hidden_parts]
    half = inner_bits - 1
    down_gram = tree_sum(last_gram(down_got, 1), dp_bits, half)
    pair_got = exchange_rows(after(pair_vector, down_got, *hidden_parts[: group // 2]))
    *partial_out, new_down = update(down_got, down_gram, 1, 2, masters[2:], ())
    pair_gram = last_gram(after(pair_got, new_down), 2)
    downs = [new_down[None]]
    for bit in range(outer_bits):
        downs = [jnp.concatenate(downs)] if len(downs) > 1 else downs
        downs = [downs[0], swapped(downs[0], "dp", inner_bits + bit)]
    downs[-1] = after(downs[-1], pair_gram)
    pair_gram = tree_sum(pair_gram, dp_bits, half)
    slot_outputs = call(
        functools.partial(project_kernel, group),
        sds((group, experts, pool, outer * block_rows), bf16),
        (my_ids, *hidden_parts, *downs),
        [smem_space] + [vmem_space] * (group + len(downs)),
        scratch=(
            pltpu.VMEM((hidden_width, total), bf16),
            pltpu.VMEM((outer * block_rows, hidden_width), bf16),
        ),
        name="project",
        vmem=12 * total * outer * block_rows + 12 * mebi,
    )
    slot_outputs = slot_outputs.reshape(group * experts, pool, outer * block_rows)
    columns = lax.all_to_all(
        slot_outputs, ("dp", "expert"), 0, 0, axis_index_groups=cubes, tiled=True
    )
    outs = update(pair_got, pair_gram, 2, 0, masters[:2], partial_out)
    forward = call(
        functools.partial(finish_kernel, experts, block_rows),
        sds((pool, width), bf16),
        (columns,),
        [vmem_space],
        name="finish",
    )
    return (*[out[None] for out in outs], forward)


def solution(mesh):
    in_specs = (
        P(("dp", "expert"), None),
        P(("dp", "expert"), None),
        P(("dp", "expert")),
        P(("dp", "expert"), None),
        P("expert", "dp", None),
        P("expert", "dp", None),
        P("expert", "dp", None),
        P("expert", None, "dp", None),
        P("expert", None, "dp", None),
    )
    out_specs = (
        P("expert", None, "dp", None),
        P("expert", None, "dp", None),
        P("expert", None, "dp", None),
        P("expert", None, "dp", None),
        P(("dp", "expert"), None),
    )
    return jax.shard_map(shards, mesh=mesh, in_specs=in_specs, out_specs=out_specs, check_vma=False)
```

```python
import functools

import jax
import jax.numpy as jnp
from jax import lax
from jax.experimental import pallas as pl
from jax.experimental.pallas import tpu as pltpu
from jax.sharding import PartitionSpec as P

first_decay = 0.9
second_decay = 0.95
learn_rate = 0.01
adam_eps = 1e-08
weight_decay = 0.1
adam_count = 100.0
norm_eps = 1e-06
gathered_limit = 16
mask_lanes = 128
mebi = 1024 * 1024
vmem_bytes = 14 * mebi
vmem_most = 56 * mebi
f32 = jnp.float32
bf16 = jnp.bfloat16
any_space = pl.BlockSpec(memory_space=pl.ANY)
smem_space = pl.BlockSpec(memory_space=pltpu.SMEM)
vmem_space = pl.BlockSpec(memory_space=pltpu.VMEM)


def swapped(array, axis, bit):
    return lax.ppermute(array, axis, [(i, i ^ 1 << bit) for i in range(lax.axis_size(axis))])


def bits_of(size):
    return size.bit_length() - 1


def cube_gather(array, steps):
    pieces = {(0, 0): array}
    for axis, bit in steps:
        for (e, k), piece in list(pieces.items()):
            key = (e ^ (1 << bit), k) if axis == "expert" else (e, k ^ (1 << bit))
            pieces[key] = swapped(piece, axis, bit)
    return pieces


def waved_gather(mine, x_rows, sent, exchange, ids):
    z = lambda value: swapped(value, "dp", 2)
    y = lambda value: swapped(value, "dp", 1)
    x = lambda value: swapped(value, "expert", 0)
    from_z, from_y, from_x = z(mine), y(mine), x(mine)
    weights = exchange(sent)
    from_z, from_y, from_x, weights = lax.optimization_barrier((from_z, from_y, from_x, weights))
    from_zy, from_zx = y(from_z), x(from_z)
    from_yx = [x(from_y[:x_rows]), y(from_x[x_rows:])]
    from_zyx = [x(from_zy[:x_rows]), y(from_zx[x_rows:])]
    from_z, from_y, from_x, mine, ids, *_ = lax.optimization_barrier(
        (from_z, from_y, from_x, mine, ids, from_zy, from_zx)
    )
    pieces = {
        (0, 0): [mine],
        (0, 4): [from_z],
        (0, 2): [from_y],
        (1, 0): [from_x],
        (0, 6): [from_zy],
        (1, 4): [from_zx],
        (1, 2): from_yx,
        (1, 6): from_zyx,
    }
    for (e, k), held in list(pieces.items()):
        pieces[e, k | 1] = [swapped(piece, "dp", 0) for piece in held]
    return pieces, weights, ids


def tree_sum(value, bits):
    for bit in bits:
        value = value + swapped(value, "dp", bit)
    return value


def nt(a, b):
    return lax.dot_general(a, b, (((1,), (1,)), ((), ())), preferred_element_type=f32)


def tn(a, b):
    return lax.dot_general(a, b, (((0,), (0,)), ((), ())), preferred_element_type=f32)


def tree_weights(entry, count):
    gram = {(i, j): entry(i, j) for i in range(count) for j in range(i, count)}
    weights = [None] * count
    size = count
    while size > 1:
        scale = []
        for j in range(0, size, 2):
            cross = gram[j, j + 1]
            scale.append(1.0 - cross / (2.0 * (gram[j, j] + norm_eps)))
            scale.append(1.0 - cross / (2.0 * (gram[j + 1, j + 1] + norm_eps)))
        span = count // size
        for leaf in range(count):
            factor = scale[leaf // span]
            weights[leaf] = factor if weights[leaf] is None else weights[leaf] * factor
        full = lambda i, j: gram[min(i, j), max(i, j)] * (scale[i] * scale[j])
        size //= 2
        if size > 1:
            gram = {
                (i, j): full(2 * i, 2 * j)
                + full(2 * i, 2 * j + 1)
                + full(2 * i + 1, 2 * j)
                + full(2 * i + 1, 2 * j + 1)
                for i in range(size)
                for j in range(i, size)
            }
    return weights


def prepare_kernel(
    route_ref, counts_ref, tok_ref, cot_ref, gate_ref, up_ref, down_ref, out_ref, sent_ref
):
    group, part = sent_ref.shape[0], sent_ref.shape[1] // 3
    for index, ref in enumerate((gate_ref, up_ref, down_ref)):
        turned = ref[...].T.astype(bf16)
        for k in range(group):
            sent_ref[k, index * part : (index + 1) * part, :] = turned[k * part : (k + 1) * part, :]
    pool, width = cot_ref.shape
    experts, capacity = route_ref.shape
    out_ref[:pool, :width] = tok_ref[...]
    out_ref[:pool, width:] = jnp.zeros((pool, mask_lanes), bf16)
    out_ref[pool:, :width] = cot_ref[...]
    ids = lax.broadcasted_iota(jnp.int32, (pool, capacity), 0)
    slots = lax.broadcasted_iota(jnp.int32, (pool, capacity), 1)
    lanes = lax.broadcasted_iota(jnp.int32, (pool, mask_lanes), 1)
    flags = jnp.zeros((pool, mask_lanes), f32)
    for e in range(experts):
        named = (ids == route_ref[e : e + 1, :]) & (slots < counts_ref[0, e])
        found = jnp.sum(named.astype(f32), axis=1, keepdims=True)
        flags = jnp.where(lanes == e, found, flags)
    out_ref[pool:, width:] = flags.astype(bf16)


def place_rows(layout, refs, into, first, lanes, rows, pool, members):
    for (e, k), held in layout.items():
        low, at = 0, k * rows + e * pool
        for index, count in held:
            begin, end = max(low, first), min(low + count, first + pool)
            if begin < end and k in members:
                source = refs[index][begin - low : end - low, :lanes]
                into[at + begin - first : at + end - first, :] = source
            low += count


def gather_kernel(layout, experts, group, pool, pieces, idx_ref, *refs):
    shared, held, refs = refs[:pieces], refs[pieces:-9], refs[-9:]
    hid_ref, hid_abs_ref, dgate_ref, dup_ref, gram_ref, x_ref, y_ref, w_ref, row_ref = refs
    slot, expert, outer_index = idx_ref[0], idx_ref[1], idx_ref[2]
    part, total = hid_ref.shape
    rows = total // group
    width = x_ref.shape[1]
    per, _, _, block_rows = held[0].shape
    for o in range(per * len(held)):
        for h, ref in enumerate(held):

            @pl.when(((outer_index ^ o) // per) == h)
            def _(ref=ref, o=o):
                source = ref.at[(outer_index ^ o) % per]
                for b in range(group):
                    at = (o * group + b) * block_rows
                    w_ref[:, at : at + block_rows] = source[b]

    row_ref[...] = jnp.zeros_like(row_ref)
    pick = lax.broadcasted_iota(jnp.int32, (8, mask_lanes), 1) == expert
    both_members = max(1, min(group, 256 // rows))
    for first in range(0, group, both_members):
        members = range(first, first + both_members)
        mine, end = slice(first * rows, (first + both_members) * rows), (first + both_members) * rows
        place_rows(layout, shared, x_ref, 0, width, rows, pool, members)
        place_rows(layout, shared, y_ref, pool, width + mask_lanes, rows, pool, members)
        pre = nt(w_ref[: 2 * part, :], x_ref[mine, :])
        outer_x = nt(x_ref[mine, :], x_ref[:end, :])
        back_hidden = nt(w_ref[2 * part :, :], y_ref[mine, :width])
        outer_y = nt(y_ref[mine, :width], y_ref[:end, :width])
        mask = nt(pick.astype(bf16), y_ref[mine, width:])[0:1] > 0.5
        gate_pre, up_pre = pre[:part], pre[part:]
        sigmoid_gate = jax.nn.sigmoid(gate_pre)
        active_gate = gate_pre * sigmoid_gate
        kept = lambda value: jnp.where(mask, value, 0.0).astype(bf16)
        hidden = kept(active_gate * up_pre)
        hid_ref[:, mine] = hidden
        for n, k in enumerate(members):
            at = pl.multiple_of((slot ^ k) * rows, rows)
            hid_abs_ref[:, pl.ds(at, rows)] = hidden[:, n * rows : (n + 1) * rows]
        dgate_ref[:, mine] = kept(
            back_hidden * up_pre * sigmoid_gate * (1.0 + gate_pre * (1.0 - sigmoid_gate))
        )
        dup_ref[:, mine] = kept(back_hidden * active_gate)
        for m, (ref, prod) in enumerate(
            ((dgate_ref, outer_x), (dup_ref, outer_x), (hid_ref, outer_y))
        ):
            both = prod * tn(ref[:, mine], ref[:, :end])
            for n, k in enumerate(members):
                sums = both[n * rows : (n + 1) * rows, : (k + 1) * rows].sum(0, keepdims=True)
                row_ref[m * group + k : m * group + k + 1, : (k + 1) * rows] = sums
    lanes = lax.broadcasted_iota(jnp.int32, gram_ref.shape, 1)
    relative = jnp.zeros(gram_ref.shape, f32)
    for k in range(group):
        sums = row_ref[:, k * rows : (k + 1) * rows].sum(1, keepdims=True)
        relative = jnp.where(lanes == (slot ^ k), sums, relative)
    row_ids = lax.broadcasted_iota(jnp.int32, gram_ref.shape, 0)
    gram = jnp.zeros(gram_ref.shape, f32)
    for m in range(3):
        for k in range(group):
            row = relative[m * group + k : m * group + k + 1]
            gram = jnp.where(row_ids == m * group + (slot ^ k), row, gram)
    gram_ref[...] = gram


def vector_kernel(group, idx_ref, gram_ref, x_ref, y_ref, dgate_ref, dup_ref, hid_ref, out_ref):
    part, total = hid_ref.shape
    rows = total // group
    count, _, block_rows = out_ref.shape
    width = count * block_rows
    slot = idx_ref[0]

    def scaled(m, ref):
        def entry(i, j):
            a, b = slot ^ i, slot ^ j
            value = gram_ref[m * group + a, b]
            if i != j:
                value = value + gram_ref[m * group + b, a]
            return jnp.full((1, rows), value, f32)

        weights = tree_weights(entry, group)
        return jnp.concatenate(
            [
                (ref[:, d * rows : (d + 1) * rows].astype(f32) * weights[d]).astype(bf16)
                for d in range(group)
            ],
            axis=1,
        )

    pair = jnp.concatenate([scaled(0, dgate_ref), scaled(1, dup_ref)], axis=0)
    vectors = (
        jnp.dot(pair, x_ref[:, :width], preferred_element_type=f32).astype(bf16),
        jnp.dot(scaled(2, hid_ref), y_ref[:, :width], preferred_element_type=f32).astype(bf16),
    )
    for i in range(count):
        lanes = slice(i * block_rows, (i + 1) * block_rows)
        out_ref[i, : 2 * part, :] = vectors[0][:, lanes]
        out_ref[i, 2 * part :, :] = vectors[1][:, lanes]


def update_kernel(group, mats, start, gram_ref, got_ref, *refs):
    masters = refs[:mats]
    first_ref, second_ref = refs[mats : mats + 2]
    outs = refs[-5:] if mats == 1 else refs[-4:]
    sum_ref, new_ref, new_first_ref, new_second_ref = outs[:4]
    outer = got_ref.shape[0] // group
    block_rows = got_ref.shape[2]
    part = got_ref.shape[1] // 3
    for m in range(mats):
        n = start + m
        entry = lambda i, j: jnp.full((1, block_rows), gram_ref[n * outer + i, j], f32)
        weights = tree_weights(entry, outer)
        total = 0.0
        for o in range(outer):
            held = [
                got_ref[o * group + s, n * part : (n + 1) * part, :].astype(f32)
                for s in range(group)
            ]
            total = total + weights[o] * jnp.concatenate(held, axis=0)
        total = total.T
        first = first_decay * first_ref[m] + (1.0 - first_decay) * total
        second = second_decay * second_ref[m] + (1.0 - second_decay) * total * total
        first_hat = first / (1.0 - first_decay**adam_count)
        second_hat = second / (1.0 - second_decay**adam_count)
        old = masters[m][...]
        new = old - learn_rate * (first_hat / (jnp.sqrt(second_hat) + adam_eps) + weight_decay * old)
        sum_ref[m] = total
        new_ref[m] = new
        new_first_ref[m] = first
        new_second_ref[m] = second
        if mats == 1:
            outs[-1][...] = new.astype(bf16)


def project_kernel(group, idx_ref, *refs):
    parts, downs, (out_ref, hidden_ref, all_ref) = refs[:group], refs[group:-3], refs[-3:]
    slot, expert, outer_index = idx_ref[0], idx_ref[1], idx_ref[2]
    bits, part = bits_of(group), parts[0].shape[0]
    for n, ref in enumerate(parts):
        relative = sum((n >> b & 1) << (bits - 1 - b) for b in range(bits))
        at = pl.multiple_of((slot ^ relative) * part, 16)
        hidden_ref[pl.ds(at, part), :] = ref[...]
    per, block_rows = downs[0].shape[:2]
    for o in range(per * len(downs)):
        for h, ref in enumerate(downs):

            @pl.when(((outer_index ^ o) // per) == h)
            def _(ref=ref, o=o):
                all_ref[o * block_rows : (o + 1) * block_rows, :] = ref[(outer_index ^ o) % per]

    made = lax.dot_general(
        hidden_ref[...], all_ref[...], (((0,), (1,)), ((), ())), preferred_element_type=f32
    )
    experts, pool = out_ref.shape[1], out_ref.shape[2]
    for d in range(out_ref.shape[0]):
        for e in range(experts):
            at = (d * experts + e) * pool
            out_ref[d, expert ^ e] = made[at : at + pool].astype(bf16)


def finish_kernel(experts, block_rows, got_ref, out_ref):
    group = got_ref.shape[0] // experts
    for o in range(got_ref.shape[2] // block_rows):
        for s in range(group):
            lanes = slice(o * block_rows, (o + 1) * block_rows)
            total = got_ref[s * experts, :, lanes].astype(f32)
            for e in range(1, experts):
                total = total + got_ref[s * experts + e, :, lanes].astype(f32)
            at = (o * group + s) * block_rows
            out_ref[:, at : at + block_rows] = total.astype(bf16)


def call(kernel, outs, args, in_specs, scratch=(), out_specs=None, aliases=None, name=None, grid=(), vmem=vmem_bytes):
    return pl.pallas_call(
        kernel,
        out_shape=outs,
        grid=grid,
        in_specs=in_specs,
        out_specs=out_specs if out_specs is not None else jax.tree.map(lambda _: vmem_space, outs),
        scratch_shapes=list(scratch),
        compiler_params=pltpu.CompilerParams(vmem_limit_bytes=min(vmem, vmem_most)),
        input_output_aliases=aliases or {},
        name=name,
    )(*args)


def after(value, *others):
    return lax.optimization_barrier((value, *others))[0]


def shards(
    tokens,
    cotangent,
    route,
    counts,
    gate_master,
    up_master,
    down_master,
    first_moment,
    second_moment,
):
    experts = lax.axis_size("expert")
    dp = lax.axis_size("dp")
    group = max(1, min(gathered_limit // experts, dp))
    inner_bits = bits_of(group)
    outer_bits = bits_of(dp // group)
    outer = dp // group
    dp_bits = inner_bits + outer_bits
    pool, width = tokens.shape
    rows = experts * pool
    total = group * rows
    block_rows, hidden_width = gate_master.shape[1:]
    part = hidden_width // group
    my_dp = lax.axis_index("dp")
    expert_index = lax.axis_index("expert")
    my_ids = jnp.stack([my_dp % group, expert_index, my_dp // group]).astype(jnp.int32)
    groups = [[o * group + s for s in range(group)] for o in range(outer)]
    cubes = [[o * group * experts + s for s in range(group * experts)] for o in range(outer)]
    capacity = route.shape[0] // experts
    sds = jax.ShapeDtypeStruct
    masters = [gate_master[0], up_master[0], down_master[0]]

    mine, sent = call(
        prepare_kernel,
        (
            sds((2 * pool, width + mask_lanes), bf16),
            sds((group, 3 * part, block_rows), bf16),
        ),
        (route.reshape(experts, capacity), counts, tokens, cotangent, *masters),
        [vmem_space, smem_space] + [vmem_space] * 5,
        name="prepare",
        vmem=vmem_most,
    )
    exchange = lambda sent: lax.all_to_all(
        sent, "dp", 0, 0, axis_index_groups=groups, tiled=True
    )
    if inner_bits == 3 and experts == 2:
        pieces, own_group, my_ids = waved_gather(
            mine, -(-5 * pool // 64) * 16, sent, exchange, my_ids
        )
    else:
        steps = [("expert", b) for b in range(bits_of(experts))]
        steps += [("dp", b) for b in reversed(range(inner_bits))]
        pieces = {key: [value] for key, value in cube_gather(mine, steps).items()}
        own_group = exchange(sent)
    shared, layout = [], {}
    for key, parts in pieces.items():
        layout[key] = [(len(shared) + n, piece.shape[0]) for n, piece in enumerate(parts)]
        shared += parts
    held = [own_group[None]]
    for bit in range(outer_bits):
        held = [jnp.concatenate(held)] if len(held) > 1 else held
        held = [held[0], swapped(held[0], "dp", inner_bits + bit)]
    wide = width + mask_lanes
    factor = sds((part, total), bf16)
    gram_rows = -(-3 * group // 8) * 8
    rows_bytes, weight_bytes = 4 * total * wide, 6 * part * width
    hidden, hidden_own, d_gate, d_up, gram, token_all, grad_all = call(
        functools.partial(gather_kernel, layout, experts, group, pool, len(shared)),
        (
            *(factor,) * 4,
            sds((gram_rows, 128), f32),
            sds((total, width), bf16),
            sds((total, wide), bf16),
        ),
        (my_ids, *shared, *held),
        [smem_space] + [vmem_space] * (len(shared) + len(held)),
        scratch=(
            pltpu.VMEM((3 * part, width), bf16),
            pltpu.VMEM((gram_rows, total), f32),
        ),
        name="forward_and_gram",
        vmem=5 * rows_bytes // 2 + 3 * weight_bytes + 4 * total * total * (outer // 4),
    )
    gram = tree_sum(gram, range(inner_bits - 1))
    hidden_parts = [hidden_own]
    for bit in reversed(range(1, inner_bits)):
        hidden_parts += [swapped(piece, "dp", bit) for piece in hidden_parts]
        gram = after(gram, hidden_parts[1]) if bit == inner_bits - 1 else gram
    gram = tree_sum(gram, range(inner_bits - 1, inner_bits))

    vector = call(
        functools.partial(vector_kernel, group),
        sds((dp, 3 * part, block_rows), bf16),
        (my_ids, gram, token_all, grad_all, d_gate, d_up, hidden),
        [smem_space] * 2 + [vmem_space] * 5,
        name="local_tree",
        vmem=5 * rows_bytes // 4 + 2 * weight_bytes + 8 * mebi,
    )
    got = lax.all_to_all(vector, "dp", 0, 0, tiled=True)
    hidden_parts = [after(piece, got) for piece in hidden_parts]
    hidden_parts += [swapped(piece, "dp", 0) for piece in hidden_parts]
    leaves = got.reshape(outer, group, 3, part, block_rows).transpose(2, 0, 1, 3, 4)
    leaves = leaves.reshape(3, outer, hidden_width, block_rows).astype(f32)
    if outer > 2:
        products = jnp.einsum("miab,mjab->mij", leaves, leaves, precision=lax.Precision.HIGHEST)
    else:
        products = (leaves[:, :, None] * leaves[:, None]).sum((3, 4))
    products = tree_sum(products.reshape(3 * outer, outer), range(dp_bits))

    def update(mats, start, olds, previous):
        place = lambda i: (start // mats, 0, 0)
        block = pl.BlockSpec((mats, block_rows, hidden_width), place)
        whole = sds((3, block_rows, hidden_width), f32)
        kernel = functools.partial(update_kernel, group, mats, start)
        outs, out_specs = (whole,) * 4, (block,) * 4
        if mats == 1:
            outs += (sds((block_rows, hidden_width), bf16),)
            out_specs += (vmem_space,)
        return call(
            kernel,
            outs,
            (products, got, *olds, first_moment[0], second_moment[0], *previous),
            [smem_space] + [vmem_space] * (1 + mats) + [block] * 2 + [any_space] * len(previous),
            out_specs=out_specs,
            aliases={4 + mats + i: i for i in range(len(previous))},
            grid=(1,),
            name="update",
            vmem=4 * got.shape[0] * got.shape[1] * 256 + 10 * mebi,
        )

    *partial_out, new_down = update(1, 2, masters[2:], ())
    downs = [new_down[None]]
    for bit in range(outer_bits):
        downs = [jnp.concatenate(downs)] if len(downs) > 1 else downs
        downs = [downs[0], swapped(downs[0], "dp", inner_bits + bit)]
    slot_outputs = call(
        functools.partial(project_kernel, group),
        sds((group, experts, pool, outer * block_rows), bf16),
        (my_ids, *hidden_parts, *downs),
        [smem_space] + [vmem_space] * (group + len(downs)),
        scratch=(
            pltpu.VMEM((hidden_width, total), bf16),
            pltpu.VMEM((outer * block_rows, hidden_width), bf16),
        ),
        name="project",
        vmem=12 * total * outer * block_rows + 12 * mebi,
    )
    slot_outputs = slot_outputs.reshape(group * experts, pool, outer * block_rows)
    columns = lax.all_to_all(
        slot_outputs, ("dp", "expert"), 0, 0, axis_index_groups=cubes, tiled=True
    )
    outs = update(2, 0, masters[:2], partial_out)
    forward = call(
        functools.partial(finish_kernel, experts, block_rows),
        sds((pool, width), bf16),
        (columns,),
        [vmem_space],
        name="finish",
    )
    return (*[out[None] for out in outs], forward)


def solution(mesh):
    in_specs = (
        P(("dp", "expert"), None),
        P(("dp", "expert"), None),
        P(("dp", "expert")),
        P(("dp", "expert"), None),
        P("expert", "dp", None),
        P("expert", "dp", None),
        P("expert", "dp", None),
        P("expert", None, "dp", None),
        P("expert", None, "dp", None),
    )
    out_specs = (
        P("expert", None, "dp", None),
        P("expert", None, "dp", None),
        P("expert", None, "dp", None),
        P("expert", None, "dp", None),
        P(("dp", "expert"), None),
    )
    return jax.shard_map(shards, mesh=mesh, in_specs=in_specs, out_specs=out_specs, check_vma=False)
```

```python
import functools

import jax
import jax.numpy as jnp
from jax import lax
from jax.experimental import pallas as pl
from jax.experimental.pallas import tpu as pltpu
from jax.sharding import PartitionSpec as P

first_decay = 0.9
second_decay = 0.95
learn_rate = 0.01
adam_eps = 1e-08
weight_decay = 0.1
adam_count = 100.0
norm_eps = 1e-06
gathered_limit = 16
mask_lanes = 128
mebi = 1024 * 1024
vmem_bytes = 14 * mebi
vmem_most = 56 * mebi
f32 = jnp.float32
bf16 = jnp.bfloat16
any_space = pl.BlockSpec(memory_space=pl.ANY)
smem_space = pl.BlockSpec(memory_space=pltpu.SMEM)
vmem_space = pl.BlockSpec(memory_space=pltpu.VMEM)


def swapped(array, axis, bit):
    return lax.ppermute(array, axis, [(i, i ^ 1 << bit) for i in range(lax.axis_size(axis))])


def bits_of(size):
    return size.bit_length() - 1


def cube_gather(array, steps):
    pieces = {(0, 0): array}
    for axis, bit in steps:
        for (e, k), piece in list(pieces.items()):
            key = (e ^ (1 << bit), k) if axis == "expert" else (e, k ^ (1 << bit))
            pieces[key] = swapped(piece, axis, bit)
    return pieces


def waved_gather(mine, x_rows, sent, exchange, ids):
    z = lambda value: swapped(value, "dp", 2)
    y = lambda value: swapped(value, "dp", 1)
    x = lambda value: swapped(value, "expert", 0)
    from_z, from_y, from_x = z(mine), y(mine), x(mine)
    weights = exchange(sent)
    from_z, from_y, from_x, weights = lax.optimization_barrier((from_z, from_y, from_x, weights))
    from_zy, from_zx = y(from_z), x(from_z)
    from_zyx = [x(from_zy[:x_rows]), y(from_zx[x_rows:])]
    from_y, from_x, from_zy, from_zx = lax.optimization_barrier((from_y, from_x, from_zy, from_zx))
    from_yx = [x(from_y[:x_rows]), y(from_x[x_rows:])]
    from_z, from_y, from_x, mine, ids, *_ = lax.optimization_barrier(
        (from_z, from_y, from_x, mine, ids, from_zy, from_zx)
    )
    pieces = {
        (0, 0): [mine],
        (0, 4): [from_z],
        (0, 2): [from_y],
        (1, 0): [from_x],
        (0, 6): [from_zy],
        (1, 4): [from_zx],
        (1, 2): from_yx,
        (1, 6): from_zyx,
    }
    for (e, k), held in list(pieces.items()):
        pieces[e, k | 1] = [swapped(piece, "dp", 0) for piece in held]
    return pieces, weights, ids


def tree_sum(value, bits):
    for bit in bits:
        value = value + swapped(value, "dp", bit)
    return value


def nt(a, b):
    return lax.dot_general(a, b, (((1,), (1,)), ((), ())), preferred_element_type=f32)


def tn(a, b):
    return lax.dot_general(a, b, (((0,), (0,)), ((), ())), preferred_element_type=f32)


def tree_weights(entry, count):
    gram = {(i, j): entry(i, j) for i in range(count) for j in range(i, count)}
    weights = [None] * count
    size = count
    while size > 1:
        scale = []
        for j in range(0, size, 2):
            cross = gram[j, j + 1]
            scale.append(1.0 - cross / (2.0 * (gram[j, j] + norm_eps)))
            scale.append(1.0 - cross / (2.0 * (gram[j + 1, j + 1] + norm_eps)))
        span = count // size
        for leaf in range(count):
            factor = scale[leaf // span]
            weights[leaf] = factor if weights[leaf] is None else weights[leaf] * factor
        full = lambda i, j: gram[min(i, j), max(i, j)] * (scale[i] * scale[j])
        size //= 2
        if size > 1:
            gram = {
                (i, j): full(2 * i, 2 * j)
                + full(2 * i, 2 * j + 1)
                + full(2 * i + 1, 2 * j)
                + full(2 * i + 1, 2 * j + 1)
                for i in range(size)
                for j in range(i, size)
            }
    return weights


def prepare_kernel(
    route_ref, counts_ref, tok_ref, cot_ref, gate_ref, up_ref, down_ref, out_ref, sent_ref
):
    group, part = sent_ref.shape[0], sent_ref.shape[1] // 3
    for index, ref in enumerate((gate_ref, up_ref, down_ref)):
        turned = ref[...].T.astype(bf16)
        for k in range(group):
            sent_ref[k, index * part : (index + 1) * part, :] = turned[k * part : (k + 1) * part, :]
    pool, width = cot_ref.shape
    experts, capacity = route_ref.shape
    out_ref[:pool, :width] = tok_ref[...]
    out_ref[:pool, width:] = jnp.zeros((pool, mask_lanes), bf16)
    out_ref[pool:, :width] = cot_ref[...]
    ids = lax.broadcasted_iota(jnp.int32, (pool, capacity), 0)
    slots = lax.broadcasted_iota(jnp.int32, (pool, capacity), 1)
    lanes = lax.broadcasted_iota(jnp.int32, (pool, mask_lanes), 1)
    flags = jnp.zeros((pool, mask_lanes), f32)
    for e in range(experts):
        named = (ids == route_ref[e : e + 1, :]) & (slots < counts_ref[0, e])
        found = jnp.sum(named.astype(f32), axis=1, keepdims=True)
        flags = jnp.where(lanes == e, found, flags)
    out_ref[pool:, width:] = flags.astype(bf16)


def place_rows(layout, refs, into, first, lanes, rows, pool, members):
    for (e, k), held in layout.items():
        low, at = 0, k * rows + e * pool
        for index, count in held:
            begin, end = max(low, first), min(low + count, first + pool)
            if begin < end and k in members:
                source = refs[index][begin - low : end - low, :lanes]
                into[at + begin - first : at + end - first, :] = source
            low += count


def gather_kernel(layout, experts, group, pool, pieces, idx_ref, *refs):
    shared, held, refs = refs[:pieces], refs[pieces:-9], refs[-9:]
    hid_ref, hid_abs_ref, dgate_ref, dup_ref, gram_ref, x_ref, y_ref, w_ref, row_ref = refs
    slot, expert, outer_index = idx_ref[0], idx_ref[1], idx_ref[2]
    part, total = hid_ref.shape
    rows = total // group
    width = x_ref.shape[1]
    per, _, _, block_rows = held[0].shape
    for o in range(per * len(held)):
        for h, ref in enumerate(held):

            @pl.when(((outer_index ^ o) // per) == h)
            def _(ref=ref, o=o):
                source = ref.at[(outer_index ^ o) % per]
                for b in range(group):
                    at = (o * group + b) * block_rows
                    w_ref[:, at : at + block_rows] = source[b]

    row_ref[...] = jnp.zeros_like(row_ref)
    pick = lax.broadcasted_iota(jnp.int32, (8, mask_lanes), 1) == expert
    both_members = max(1, min(group, 256 // rows))
    for first in range(0, group, both_members):
        members = range(first, first + both_members)
        mine, end = slice(first * rows, (first + both_members) * rows), (first + both_members) * rows
        place_rows(layout, shared, x_ref, 0, width, rows, pool, members)
        place_rows(layout, shared, y_ref, pool, width + mask_lanes, rows, pool, members)
        pre = nt(w_ref[: 2 * part, :], x_ref[mine, :])
        outer_x = nt(x_ref[mine, :], x_ref[:end, :])
        back_hidden = nt(w_ref[2 * part :, :], y_ref[mine, :width])
        outer_y = nt(y_ref[mine, :width], y_ref[:end, :width])
        mask = nt(pick.astype(bf16), y_ref[mine, width:])[0:1] > 0.5
        gate_pre, up_pre = pre[:part], pre[part:]
        sigmoid_gate = jax.nn.sigmoid(gate_pre)
        active_gate = gate_pre * sigmoid_gate
        kept = lambda value: jnp.where(mask, value, 0.0).astype(bf16)
        hidden = kept(active_gate * up_pre)
        hid_ref[:, mine] = hidden
        for n, k in enumerate(members):
            at = pl.multiple_of((slot ^ k) * rows, rows)
            hid_abs_ref[:, pl.ds(at, rows)] = hidden[:, n * rows : (n + 1) * rows]
        dgate_ref[:, mine] = kept(
            back_hidden * up_pre * sigmoid_gate * (1.0 + gate_pre * (1.0 - sigmoid_gate))
        )
        dup_ref[:, mine] = kept(back_hidden * active_gate)
        for m, (ref, prod) in enumerate(
            ((dgate_ref, outer_x), (dup_ref, outer_x), (hid_ref, outer_y))
        ):
            both = prod * tn(ref[:, mine], ref[:, :end])
            for n, k in enumerate(members):
                sums = both[n * rows : (n + 1) * rows, : (k + 1) * rows].sum(0, keepdims=True)
                row_ref[m * group + k : m * group + k + 1, : (k + 1) * rows] = sums
    lanes = lax.broadcasted_iota(jnp.int32, gram_ref.shape, 1)
    relative = jnp.zeros(gram_ref.shape, f32)
    for k in range(group):
        sums = row_ref[:, k * rows : (k + 1) * rows].sum(1, keepdims=True)
        relative = jnp.where(lanes == (slot ^ k), sums, relative)
    row_ids = lax.broadcasted_iota(jnp.int32, gram_ref.shape, 0)
    gram = jnp.zeros(gram_ref.shape, f32)
    for m in range(3):
        for k in range(group):
            row = relative[m * group + k : m * group + k + 1]
            gram = jnp.where(row_ids == m * group + (slot ^ k), row, gram)
    gram_ref[...] = gram


def vector_kernel(group, idx_ref, gram_ref, x_ref, y_ref, dgate_ref, dup_ref, hid_ref, out_ref):
    part, total = hid_ref.shape
    rows = total // group
    count, _, block_rows = out_ref.shape
    width = count * block_rows
    slot = idx_ref[0]

    def scaled(m, ref):
        def entry(i, j):
            a, b = slot ^ i, slot ^ j
            value = gram_ref[m * group + a, b]
            if i != j:
                value = value + gram_ref[m * group + b, a]
            return jnp.full((1, rows), value, f32)

        weights = tree_weights(entry, group)
        return jnp.concatenate(
            [
                (ref[:, d * rows : (d + 1) * rows].astype(f32) * weights[d]).astype(bf16)
                for d in range(group)
            ],
            axis=1,
        )

    pair = jnp.concatenate([scaled(0, dgate_ref), scaled(1, dup_ref)], axis=0)
    vectors = (
        jnp.dot(pair, x_ref[:, :width], preferred_element_type=f32).astype(bf16),
        jnp.dot(scaled(2, hid_ref), y_ref[:, :width], preferred_element_type=f32).astype(bf16),
    )
    for i in range(count):
        lanes = slice(i * block_rows, (i + 1) * block_rows)
        out_ref[i, : 2 * part, :] = vectors[0][:, lanes]
        out_ref[i, 2 * part :, :] = vectors[1][:, lanes]


def update_kernel(group, mats, start, gram_ref, got_ref, *refs):
    masters = refs[:mats]
    first_ref, second_ref = refs[mats : mats + 2]
    outs = refs[-5:] if mats == 1 else refs[-4:]
    sum_ref, new_ref, new_first_ref, new_second_ref = outs[:4]
    outer = got_ref.shape[0] // group
    block_rows = got_ref.shape[2]
    part = got_ref.shape[1] // 3
    for m in range(mats):
        n = start + m
        entry = lambda i, j: jnp.full((1, block_rows), gram_ref[n * outer + i, j], f32)
        weights = tree_weights(entry, outer)
        total = 0.0
        for o in range(outer):
            held = [
                got_ref[o * group + s, n * part : (n + 1) * part, :].astype(f32)
                for s in range(group)
            ]
            total = total + weights[o] * jnp.concatenate(held, axis=0)
        total = total.T
        first = first_decay * first_ref[m] + (1.0 - first_decay) * total
        second = second_decay * second_ref[m] + (1.0 - second_decay) * total * total
        first_hat = first / (1.0 - first_decay**adam_count)
        second_hat = second / (1.0 - second_decay**adam_count)
        old = masters[m][...]
        new = old - learn_rate * (first_hat / (jnp.sqrt(second_hat) + adam_eps) + weight_decay * old)
        sum_ref[m] = total
        new_ref[m] = new
        new_first_ref[m] = first
        new_second_ref[m] = second
        if mats == 1:
            outs[-1][...] = new.astype(bf16)


def project_kernel(group, idx_ref, *refs):
    parts, downs, (out_ref, hidden_ref, all_ref) = refs[:group], refs[group:-3], refs[-3:]
    slot, expert, outer_index = idx_ref[0], idx_ref[1], idx_ref[2]
    bits, part = bits_of(group), parts[0].shape[0]
    for n, ref in enumerate(parts):
        relative = sum((n >> b & 1) << (bits - 1 - b) for b in range(bits))
        at = pl.multiple_of((slot ^ relative) * part, 16)
        hidden_ref[pl.ds(at, part), :] = ref[...]
    per, block_rows = downs[0].shape[:2]
    for o in range(per * len(downs)):
        for h, ref in enumerate(downs):

            @pl.when(((outer_index ^ o) // per) == h)
            def _(ref=ref, o=o):
                all_ref[o * block_rows : (o + 1) * block_rows, :] = ref[(outer_index ^ o) % per]

    made = lax.dot_general(
        hidden_ref[...], all_ref[...], (((0,), (1,)), ((), ())), preferred_element_type=f32
    )
    experts, pool = out_ref.shape[1], out_ref.shape[2]
    for d in range(out_ref.shape[0]):
        for e in range(experts):
            at = (d * experts + e) * pool
            out_ref[d, expert ^ e] = made[at : at + pool].astype(bf16)


def finish_kernel(experts, block_rows, got_ref, out_ref):
    group = got_ref.shape[0] // experts
    for o in range(got_ref.shape[2] // block_rows):
        for s in range(group):
            lanes = slice(o * block_rows, (o + 1) * block_rows)
            total = got_ref[s * experts, :, lanes].astype(f32)
            for e in range(1, experts):
                total = total + got_ref[s * experts + e, :, lanes].astype(f32)
            at = (o * group + s) * block_rows
            out_ref[:, at : at + block_rows] = total.astype(bf16)


def call(kernel, outs, args, in_specs, scratch=(), out_specs=None, aliases=None, name=None, grid=(), vmem=vmem_bytes):
    return pl.pallas_call(
        kernel,
        out_shape=outs,
        grid=grid,
        in_specs=in_specs,
        out_specs=out_specs if out_specs is not None else jax.tree.map(lambda _: vmem_space, outs),
        scratch_shapes=list(scratch),
        compiler_params=pltpu.CompilerParams(vmem_limit_bytes=min(vmem, vmem_most)),
        input_output_aliases=aliases or {},
        name=name,
    )(*args)


def after(value, *others):
    return lax.optimization_barrier((value, *others))[0]


def shards(
    tokens,
    cotangent,
    route,
    counts,
    gate_master,
    up_master,
    down_master,
    first_moment,
    second_moment,
):
    experts = lax.axis_size("expert")
    dp = lax.axis_size("dp")
    group = max(1, min(gathered_limit // experts, dp))
    inner_bits = bits_of(group)
    outer_bits = bits_of(dp // group)
    outer = dp // group
    dp_bits = inner_bits + outer_bits
    pool, width = tokens.shape
    rows = experts * pool
    total = group * rows
    block_rows, hidden_width = gate_master.shape[1:]
    part = hidden_width // group
    my_dp = lax.axis_index("dp")
    expert_index = lax.axis_index("expert")
    my_ids = jnp.stack([my_dp % group, expert_index, my_dp // group]).astype(jnp.int32)
    groups = [[o * group + s for s in range(group)] for o in range(outer)]
    cubes = [[o * group * experts + s for s in range(group * experts)] for o in range(outer)]
    capacity = route.shape[0] // experts
    sds = jax.ShapeDtypeStruct
    masters = [gate_master[0], up_master[0], down_master[0]]

    mine, sent = call(
        prepare_kernel,
        (
            sds((2 * pool, width + mask_lanes), bf16),
            sds((group, 3 * part, block_rows), bf16),
        ),
        (route.reshape(experts, capacity), counts, tokens, cotangent, *masters),
        [vmem_space, smem_space] + [vmem_space] * 5,
        name="prepare",
        vmem=vmem_most,
    )
    exchange = lambda sent: lax.all_to_all(
        sent, "dp", 0, 0, axis_index_groups=groups, tiled=True
    )
    if inner_bits == 3 and experts == 2:
        pieces, own_group, my_ids = waved_gather(
            mine, -(-4 * pool // 64) * 16, sent, exchange, my_ids
        )
    else:
        steps = [("expert", b) for b in range(bits_of(experts))]
        steps += [("dp", b) for b in reversed(range(inner_bits))]
        pieces = {key: [value] for key, value in cube_gather(mine, steps).items()}
        own_group = exchange(sent)
    shared, layout = [], {}
    for key, parts in pieces.items():
        layout[key] = [(len(shared) + n, piece.shape[0]) for n, piece in enumerate(parts)]
        shared += parts
    held = [own_group[None]]
    for bit in range(outer_bits):
        held = [jnp.concatenate(held)] if len(held) > 1 else held
        held = [held[0], swapped(held[0], "dp", inner_bits + bit)]
    wide = width + mask_lanes
    factor = sds((part, total), bf16)
    gram_rows = -(-3 * group // 8) * 8
    rows_bytes, weight_bytes = 4 * total * wide, 6 * part * width
    hidden, hidden_own, d_gate, d_up, gram, token_all, grad_all = call(
        functools.partial(gather_kernel, layout, experts, group, pool, len(shared)),
        (
            *(factor,) * 4,
            sds((gram_rows, 128), f32),
            sds((total, width), bf16),
            sds((total, wide), bf16),
        ),
        (my_ids, *shared, *held),
        [smem_space] + [vmem_space] * (len(shared) + len(held)),
        scratch=(
            pltpu.VMEM((3 * part, width), bf16),
            pltpu.VMEM((gram_rows, total), f32),
        ),
        name="forward_and_gram",
        vmem=5 * rows_bytes // 2 + 3 * weight_bytes + 4 * total * total * (outer // 4),
    )
    gram = tree_sum(gram, range(inner_bits - 1))
    hidden_parts = [hidden_own]
    for bit in reversed(range(1, inner_bits)):
        hidden_parts += [swapped(piece, "dp", bit) for piece in hidden_parts]
        gram = after(gram, hidden_parts[1]) if bit == inner_bits - 1 else gram
    gram = tree_sum(gram, range(inner_bits - 1, inner_bits))

    vector = call(
        functools.partial(vector_kernel, group),
        sds((dp, 3 * part, block_rows), bf16),
        (my_ids, gram, token_all, grad_all, d_gate, d_up, hidden),
        [smem_space] * 2 + [vmem_space] * 5,
        name="local_tree",
        vmem=5 * rows_bytes // 4 + 2 * weight_bytes + 8 * mebi,
    )
    got = lax.all_to_all(vector, "dp", 0, 0, tiled=True)
    hidden_parts = [after(piece, got) for piece in hidden_parts]
    hidden_parts += [swapped(piece, "dp", 0) for piece in hidden_parts]
    leaves = got.reshape(outer, group, 3, part, block_rows).transpose(2, 0, 1, 3, 4)
    leaves = leaves.reshape(3, outer, hidden_width, block_rows).astype(f32)
    if outer > 2:
        products = jnp.einsum("miab,mjab->mij", leaves, leaves, precision=lax.Precision.HIGHEST)
    else:
        products = (leaves[:, :, None] * leaves[:, None]).sum((3, 4))
    products = tree_sum(products.reshape(3 * outer, outer), range(dp_bits))

    def update(mats, start, olds, previous):
        place = lambda i: (start // mats, 0, 0)
        block = pl.BlockSpec((mats, block_rows, hidden_width), place)
        whole = sds((3, block_rows, hidden_width), f32)
        kernel = functools.partial(update_kernel, group, mats, start)
        outs, out_specs = (whole,) * 4, (block,) * 4
        if mats == 1:
            outs += (sds((block_rows, hidden_width), bf16),)
            out_specs += (vmem_space,)
        return call(
            kernel,
            outs,
            (products, got, *olds, first_moment[0], second_moment[0], *previous),
            [smem_space] + [vmem_space] * (1 + mats) + [block] * 2 + [any_space] * len(previous),
            out_specs=out_specs,
            aliases={4 + mats + i: i for i in range(len(previous))},
            grid=(1,),
            name="update",
            vmem=4 * got.shape[0] * got.shape[1] * 256 + 10 * mebi,
        )

    *partial_out, new_down = update(1, 2, masters[2:], ())
    downs = [new_down[None]]
    for bit in range(outer_bits):
        downs = [jnp.concatenate(downs)] if len(downs) > 1 else downs
        downs = [downs[0], swapped(downs[0], "dp", inner_bits + bit)]
    slot_outputs = call(
        functools.partial(project_kernel, group),
        sds((group, experts, pool, outer * block_rows), bf16),
        (my_ids, *hidden_parts, *downs),
        [smem_space] + [vmem_space] * (group + len(downs)),
        scratch=(
            pltpu.VMEM((hidden_width, total), bf16),
            pltpu.VMEM((outer * block_rows, hidden_width), bf16),
        ),
        name="project",
        vmem=12 * total * outer * block_rows + 12 * mebi,
    )
    slot_outputs = slot_outputs.reshape(group * experts, pool, outer * block_rows)
    columns = lax.all_to_all(
        slot_outputs, ("dp", "expert"), 0, 0, axis_index_groups=cubes, tiled=True
    )
    outs = update(2, 0, masters[:2], partial_out)
    forward = call(
        functools.partial(finish_kernel, experts, block_rows),
        sds((pool, width), bf16),
        (columns,),
        [vmem_space],
        name="finish",
    )
    return (*[out[None] for out in outs], forward)


def solution(mesh):
    in_specs = (
        P(("dp", "expert"), None),
        P(("dp", "expert"), None),
        P(("dp", "expert")),
        P(("dp", "expert"), None),
        P("expert", "dp", None),
        P("expert", "dp", None),
        P("expert", "dp", None),
        P("expert", None, "dp", None),
        P("expert", None, "dp", None),
    )
    out_specs = (
        P("expert", None, "dp", None),
        P("expert", None, "dp", None),
        P("expert", None, "dp", None),
        P("expert", None, "dp", None),
        P(("dp", "expert"), None),
    )
    return jax.shard_map(shards, mesh=mesh, in_specs=in_specs, out_specs=out_specs, check_vma=False)
```

```python
import functools

import jax
import jax.numpy as jnp
from jax import lax
from jax.experimental import pallas as pl
from jax.experimental.pallas import tpu as pltpu
from jax.sharding import PartitionSpec as P

first_decay = 0.9
second_decay = 0.95
learn_rate = 0.01
adam_eps = 1e-08
weight_decay = 0.1
adam_count = 100.0
norm_eps = 1e-06
gathered_limit = 16
mask_lanes = 128
mebi = 1024 * 1024
vmem_bytes = 14 * mebi
vmem_most = 56 * mebi
f32 = jnp.float32
bf16 = jnp.bfloat16
any_space = pl.BlockSpec(memory_space=pl.ANY)
smem_space = pl.BlockSpec(memory_space=pltpu.SMEM)
vmem_space = pl.BlockSpec(memory_space=pltpu.VMEM)


def swapped(array, axis, bit):
    return lax.ppermute(array, axis, [(i, i ^ 1 << bit) for i in range(lax.axis_size(axis))])


def bits_of(size):
    return size.bit_length() - 1


def cube_gather(array, steps):
    pieces = {(0, 0): array}
    for axis, bit in steps:
        for (e, k), piece in list(pieces.items()):
            key = (e ^ (1 << bit), k) if axis == "expert" else (e, k ^ (1 << bit))
            pieces[key] = swapped(piece, axis, bit)
    return pieces


def waved_gather(mine, x_rows, sent, exchange, ids):
    z = lambda value: swapped(value, "dp", 2)
    y = lambda value: swapped(value, "dp", 1)
    x = lambda value: swapped(value, "expert", 0)
    from_z, from_y, from_x = z(mine), y(mine), x(mine)
    weights = exchange(sent)
    from_z, from_y, from_x, weights = lax.optimization_barrier((from_z, from_y, from_x, weights))
    from_zy, from_zx = y(from_z), x(from_z)
    from_zyx = [x(from_zy[:x_rows]), y(from_zx[x_rows:])]
    from_y, from_x, from_zy, from_zx = lax.optimization_barrier((from_y, from_x, from_zy, from_zx))
    from_yx = [x(from_y[:x_rows]), y(from_x[x_rows:])]
    from_z, from_y, from_x, mine, ids, *_ = lax.optimization_barrier(
        (from_z, from_y, from_x, mine, ids, from_zy, from_zx)
    )
    pieces = {
        (0, 0): [mine],
        (0, 4): [from_z],
        (0, 2): [from_y],
        (1, 0): [from_x],
        (0, 6): [from_zy],
        (1, 4): [from_zx],
        (1, 2): from_yx,
        (1, 6): from_zyx,
    }
    for (e, k), held in list(pieces.items()):
        pieces[e, k | 1] = [swapped(piece, "dp", 0) for piece in held]
    return pieces, weights, ids


def tree_sum(value, bits):
    for bit in bits:
        value = value + swapped(value, "dp", bit)
    return value


def nt(a, b):
    return lax.dot_general(a, b, (((1,), (1,)), ((), ())), preferred_element_type=f32)


def tn(a, b):
    return lax.dot_general(a, b, (((0,), (0,)), ((), ())), preferred_element_type=f32)


def tree_weights(entry, count):
    gram = {(i, j): entry(i, j) for i in range(count) for j in range(i, count)}
    weights = [None] * count
    size = count
    while size > 1:
        scale = []
        for j in range(0, size, 2):
            cross = gram[j, j + 1]
            scale.append(1.0 - cross / (2.0 * (gram[j, j] + norm_eps)))
            scale.append(1.0 - cross / (2.0 * (gram[j + 1, j + 1] + norm_eps)))
        span = count // size
        for leaf in range(count):
            factor = scale[leaf // span]
            weights[leaf] = factor if weights[leaf] is None else weights[leaf] * factor
        full = lambda i, j: gram[min(i, j), max(i, j)] * (scale[i] * scale[j])
        size //= 2
        if size > 1:
            gram = {
                (i, j): full(2 * i, 2 * j)
                + full(2 * i, 2 * j + 1)
                + full(2 * i + 1, 2 * j)
                + full(2 * i + 1, 2 * j + 1)
                for i in range(size)
                for j in range(i, size)
            }
    return weights


def prepare_kernel(
    route_ref, counts_ref, tok_ref, cot_ref, gate_ref, up_ref, down_ref, out_ref, sent_ref
):
    group, part = sent_ref.shape[0], sent_ref.shape[1] // 3
    for index, ref in enumerate((gate_ref, up_ref, down_ref)):
        turned = ref[...].T.astype(bf16)
        for k in range(group):
            sent_ref[k, index * part : (index + 1) * part, :] = turned[k * part : (k + 1) * part, :]
    pool, width = cot_ref.shape
    experts, capacity = route_ref.shape
    out_ref[:pool, :width] = tok_ref[...]
    out_ref[:pool, width:] = jnp.zeros((pool, mask_lanes), bf16)
    out_ref[pool:, :width] = cot_ref[...]
    ids = lax.broadcasted_iota(jnp.int32, (pool, capacity), 0)
    slots = lax.broadcasted_iota(jnp.int32, (pool, capacity), 1)
    lanes = lax.broadcasted_iota(jnp.int32, (pool, mask_lanes), 1)
    flags = jnp.zeros((pool, mask_lanes), f32)
    for e in range(experts):
        named = (ids == route_ref[e : e + 1, :]) & (slots < counts_ref[0, e])
        found = jnp.sum(named.astype(f32), axis=1, keepdims=True)
        flags = jnp.where(lanes == e, found, flags)
    out_ref[pool:, width:] = flags.astype(bf16)


def place_rows(layout, refs, into, first, lanes, rows, pool, members):
    for (e, k), held in layout.items():
        low, at = 0, k * rows + e * pool
        for index, count in held:
            begin, end = max(low, first), min(low + count, first + pool)
            if begin < end and k in members:
                source = refs[index][begin - low : end - low, :lanes]
                into[at + begin - first : at + end - first, :] = source
            low += count


def gather_kernel(layout, experts, group, pool, pieces, idx_ref, *refs):
    shared, held, refs = refs[:pieces], refs[pieces:-9], refs[-9:]
    hid_ref, hid_abs_ref, dgate_ref, dup_ref, gram_ref, x_ref, y_ref, w_ref, row_ref = refs
    slot, expert, outer_index = idx_ref[0], idx_ref[1], idx_ref[2]
    part, total = hid_ref.shape
    rows = total // group
    width = x_ref.shape[1]
    per, _, _, block_rows = held[0].shape
    for o in range(per * len(held)):
        for h, ref in enumerate(held):

            @pl.when(((outer_index ^ o) // per) == h)
            def _(ref=ref, o=o):
                source = ref.at[(outer_index ^ o) % per]
                for b in range(group):
                    at = (o * group + b) * block_rows
                    w_ref[:, at : at + block_rows] = source[b]

    row_ref[...] = jnp.zeros_like(row_ref)
    pick = lax.broadcasted_iota(jnp.int32, (8, mask_lanes), 1) == expert
    both_members = max(1, min(group, 256 // rows))
    for first in range(0, group, both_members):
        members = range(first, first + both_members)
        mine, end = slice(first * rows, (first + both_members) * rows), (first + both_members) * rows
        place_rows(layout, shared, x_ref, 0, width, rows, pool, members)
        place_rows(layout, shared, y_ref, pool, width + mask_lanes, rows, pool, members)
        pre = nt(w_ref[: 2 * part, :], x_ref[mine, :])
        outer_x = nt(x_ref[mine, :], x_ref[:end, :])
        back_hidden = nt(w_ref[2 * part :, :], y_ref[mine, :width])
        outer_y = nt(y_ref[mine, :width], y_ref[:end, :width])
        mask = nt(pick.astype(bf16), y_ref[mine, width:])[0:1] > 0.5
        gate_pre, up_pre = pre[:part], pre[part:]
        sigmoid_gate = jax.nn.sigmoid(gate_pre)
        active_gate = gate_pre * sigmoid_gate
        kept = lambda value: jnp.where(mask, value, 0.0).astype(bf16)
        hidden = kept(active_gate * up_pre)
        hid_ref[:, mine] = hidden
        for n, k in enumerate(members):
            at = pl.multiple_of((slot ^ k) * rows, rows)
            hid_abs_ref[:, pl.ds(at, rows)] = hidden[:, n * rows : (n + 1) * rows]
        dgate_ref[:, mine] = kept(
            back_hidden * up_pre * sigmoid_gate * (1.0 + gate_pre * (1.0 - sigmoid_gate))
        )
        dup_ref[:, mine] = kept(back_hidden * active_gate)
        for m, (ref, prod) in enumerate(
            ((dgate_ref, outer_x), (dup_ref, outer_x), (hid_ref, outer_y))
        ):
            both = prod * tn(ref[:, mine], ref[:, :end])
            for n, k in enumerate(members):
                sums = both[n * rows : (n + 1) * rows, : (k + 1) * rows].sum(0, keepdims=True)
                row_ref[m * group + k : m * group + k + 1, : (k + 1) * rows] = sums
    lanes = lax.broadcasted_iota(jnp.int32, gram_ref.shape, 1)
    relative = jnp.zeros(gram_ref.shape, f32)
    for k in range(group):
        sums = row_ref[:, k * rows : (k + 1) * rows].sum(1, keepdims=True)
        relative = jnp.where(lanes == (slot ^ k), sums, relative)
    row_ids = lax.broadcasted_iota(jnp.int32, gram_ref.shape, 0)
    gram = jnp.zeros(gram_ref.shape, f32)
    for m in range(3):
        for k in range(group):
            row = relative[m * group + k : m * group + k + 1]
            gram = jnp.where(row_ids == m * group + (slot ^ k), row, gram)
    gram_ref[...] = gram


def vector_kernel(group, idx_ref, gram_ref, x_ref, y_ref, dgate_ref, dup_ref, hid_ref, out_ref):
    part, total = hid_ref.shape
    rows = total // group
    count, _, block_rows = out_ref.shape
    width = count * block_rows
    slot = idx_ref[0]

    def scaled(m, ref):
        def entry(i, j):
            a, b = slot ^ i, slot ^ j
            value = gram_ref[m * group + a, b]
            if i != j:
                value = value + gram_ref[m * group + b, a]
            return jnp.full((1, rows), value, f32)

        weights = tree_weights(entry, group)
        return jnp.concatenate(
            [
                (ref[:, d * rows : (d + 1) * rows].astype(f32) * weights[d]).astype(bf16)
                for d in range(group)
            ],
            axis=1,
        )

    pair = jnp.concatenate([scaled(0, dgate_ref), scaled(1, dup_ref)], axis=0)
    vectors = (
        jnp.dot(pair, x_ref[:, :width], preferred_element_type=f32).astype(bf16),
        jnp.dot(scaled(2, hid_ref), y_ref[:, :width], preferred_element_type=f32).astype(bf16),
    )
    for i in range(count):
        lanes = slice(i * block_rows, (i + 1) * block_rows)
        out_ref[i, : 2 * part, :] = vectors[0][:, lanes]
        out_ref[i, 2 * part :, :] = vectors[1][:, lanes]


def update_kernel(group, mats, start, gram_ref, got_ref, *refs):
    masters = refs[:mats]
    first_ref, second_ref = refs[mats : mats + 2]
    outs = refs[-5:] if mats == 1 else refs[-4:]
    sum_ref, new_ref, new_first_ref, new_second_ref = outs[:4]
    outer = got_ref.shape[0] // group
    block_rows = got_ref.shape[2]
    part = got_ref.shape[1] // 3
    for m in range(mats):
        n = start + m
        entry = lambda i, j: jnp.full((1, block_rows), gram_ref[n * outer + i, j], f32)
        weights = tree_weights(entry, outer)
        total = 0.0
        for o in range(outer):
            held = [
                got_ref[o * group + s, n * part : (n + 1) * part, :].astype(f32)
                for s in range(group)
            ]
            total = total + weights[o] * jnp.concatenate(held, axis=0)
        total = total.T
        first = first_decay * first_ref[m] + (1.0 - first_decay) * total
        second = second_decay * second_ref[m] + (1.0 - second_decay) * total * total
        first_hat = first / (1.0 - first_decay**adam_count)
        second_hat = second / (1.0 - second_decay**adam_count)
        old = masters[m][...]
        new = old - learn_rate * (first_hat / (jnp.sqrt(second_hat) + adam_eps) + weight_decay * old)
        sum_ref[m] = total
        new_ref[m] = new
        new_first_ref[m] = first
        new_second_ref[m] = second
        if mats == 1:
            outs[-1][...] = new.astype(bf16)


def project_kernel(group, idx_ref, *refs):
    parts, downs, (out_ref, hidden_ref, all_ref) = refs[:group], refs[group:-3], refs[-3:]
    slot, expert, outer_index = idx_ref[0], idx_ref[1], idx_ref[2]
    bits, part = bits_of(group), parts[0].shape[0]
    for n, ref in enumerate(parts):
        relative = sum((n >> b & 1) << (bits - 1 - b) for b in range(bits))
        at = pl.multiple_of((slot ^ relative) * part, 16)
        hidden_ref[pl.ds(at, part), :] = ref[...]
    per, block_rows = downs[0].shape[:2]
    for o in range(per * len(downs)):
        for h, ref in enumerate(downs):

            @pl.when(((outer_index ^ o) // per) == h)
            def _(ref=ref, o=o):
                all_ref[o * block_rows : (o + 1) * block_rows, :] = ref[(outer_index ^ o) % per]

    made = lax.dot_general(
        hidden_ref[...], all_ref[...], (((0,), (1,)), ((), ())), preferred_element_type=f32
    )
    experts, pool = out_ref.shape[1], out_ref.shape[2]
    for d in range(out_ref.shape[0]):
        for e in range(experts):
            at = (d * experts + e) * pool
            out_ref[d, expert ^ e] = made[at : at + pool].astype(bf16)


def finish_kernel(experts, block_rows, got_ref, out_ref):
    group = got_ref.shape[0] // experts
    for o in range(got_ref.shape[2] // block_rows):
        for s in range(group):
            lanes = slice(o * block_rows, (o + 1) * block_rows)
            total = got_ref[s * experts, :, lanes].astype(f32)
            for e in range(1, experts):
                total = total + got_ref[s * experts + e, :, lanes].astype(f32)
            at = (o * group + s) * block_rows
            out_ref[:, at : at + block_rows] = total.astype(bf16)


def call(kernel, outs, args, in_specs, scratch=(), out_specs=None, aliases=None, name=None, grid=(), vmem=vmem_bytes):
    return pl.pallas_call(
        kernel,
        out_shape=outs,
        grid=grid,
        in_specs=in_specs,
        out_specs=out_specs if out_specs is not None else jax.tree.map(lambda _: vmem_space, outs),
        scratch_shapes=list(scratch),
        compiler_params=pltpu.CompilerParams(vmem_limit_bytes=min(vmem, vmem_most)),
        input_output_aliases=aliases or {},
        name=name,
    )(*args)


def after(value, *others):
    return lax.optimization_barrier((value, *others))[0]


def shards(
    tokens,
    cotangent,
    route,
    counts,
    gate_master,
    up_master,
    down_master,
    first_moment,
    second_moment,
):
    experts = lax.axis_size("expert")
    dp = lax.axis_size("dp")
    group = max(1, min(gathered_limit // experts, dp))
    inner_bits = bits_of(group)
    outer_bits = bits_of(dp // group)
    outer = dp // group
    dp_bits = inner_bits + outer_bits
    pool, width = tokens.shape
    rows = experts * pool
    total = group * rows
    block_rows, hidden_width = gate_master.shape[1:]
    part = hidden_width // group
    my_dp = lax.axis_index("dp")
    expert_index = lax.axis_index("expert")
    my_ids = jnp.stack([my_dp % group, expert_index, my_dp // group]).astype(jnp.int32)
    groups = [[o * group + s for s in range(group)] for o in range(outer)]
    cubes = [[o * group * experts + s for s in range(group * experts)] for o in range(outer)]
    capacity = route.shape[0] // experts
    sds = jax.ShapeDtypeStruct
    masters = [gate_master[0], up_master[0], down_master[0]]

    mine, sent = call(
        prepare_kernel,
        (
            sds((2 * pool, width + mask_lanes), bf16),
            sds((group, 3 * part, block_rows), bf16),
        ),
        (route.reshape(experts, capacity), counts, tokens, cotangent, *masters),
        [vmem_space, smem_space] + [vmem_space] * 5,
        name="prepare",
        vmem=vmem_most,
    )
    exchange = lambda sent: lax.all_to_all(
        sent, "dp", 0, 0, axis_index_groups=groups, tiled=True
    )
    if inner_bits == 3 and experts == 2:
        pieces, own_group, my_ids = waved_gather(
            mine, -(-4 * pool // 64) * 16, sent, exchange, my_ids
        )
    else:
        steps = [("expert", b) for b in range(bits_of(experts))]
        steps += [("dp", b) for b in reversed(range(inner_bits))]
        pieces = {key: [value] for key, value in cube_gather(mine, steps).items()}
        own_group = exchange(sent)
    shared, layout = [], {}
    for key, parts in pieces.items():
        layout[key] = [(len(shared) + n, piece.shape[0]) for n, piece in enumerate(parts)]
        shared += parts
    held = [own_group[None]]
    for bit in range(outer_bits):
        held = [jnp.concatenate(held)] if len(held) > 1 else held
        held = [held[0], swapped(held[0], "dp", inner_bits + bit)]
    wide = width + mask_lanes
    factor = sds((part, total), bf16)
    gram_rows = -(-3 * group // 8) * 8
    rows_bytes, weight_bytes = 4 * total * wide, 6 * part * width
    hidden, hidden_own, d_gate, d_up, gram, token_all, grad_all = call(
        functools.partial(gather_kernel, layout, experts, group, pool, len(shared)),
        (
            *(factor,) * 4,
            sds((gram_rows, 128), f32),
            sds((total, width), bf16),
            sds((total, wide), bf16),
        ),
        (my_ids, *shared, *held),
        [smem_space] + [vmem_space] * (len(shared) + len(held)),
        scratch=(
            pltpu.VMEM((3 * part, width), bf16),
            pltpu.VMEM((gram_rows, total), f32),
        ),
        name="forward_and_gram",
        vmem=5 * rows_bytes // 2 + 3 * weight_bytes + 4 * total * total * (outer // 4),
    )
    gram = tree_sum(gram, range(inner_bits - 1))
    hidden_parts = [hidden_own]
    for bit in reversed(range(1, inner_bits)):
        hidden_parts += [swapped(piece, "dp", bit) for piece in hidden_parts]
        gram = after(gram, hidden_parts[1]) if bit == inner_bits - 1 else gram
    gram = tree_sum(gram, range(inner_bits - 1, inner_bits))

    vector = call(
        functools.partial(vector_kernel, group),
        sds((dp, 3 * part, block_rows), bf16),
        (my_ids, gram, token_all, grad_all, d_gate, d_up, hidden),
        [smem_space] * 2 + [vmem_space] * 5,
        name="local_tree",
        vmem=5 * rows_bytes // 4 + 2 * weight_bytes + 8 * mebi,
    )
    got = lax.all_to_all(vector, "dp", 0, 0, tiled=True)
    hidden_parts += [swapped(piece, "dp", 0) for piece in hidden_parts]
    leaves = got.reshape(outer, group, 3, part, block_rows).transpose(2, 0, 1, 3, 4)
    leaves = leaves.reshape(3, outer, hidden_width, block_rows).astype(f32)
    if outer > 2:
        products = jnp.einsum("miab,mjab->mij", leaves, leaves, precision=lax.Precision.HIGHEST)
    else:
        products = (leaves[:, :, None] * leaves[:, None]).sum((3, 4))
    products = tree_sum(products.reshape(3 * outer, outer), range(dp_bits))

    def update(mats, start, olds, previous):
        place = lambda i: (start // mats, 0, 0)
        block = pl.BlockSpec((mats, block_rows, hidden_width), place)
        whole = sds((3, block_rows, hidden_width), f32)
        kernel = functools.partial(update_kernel, group, mats, start)
        outs, out_specs = (whole,) * 4, (block,) * 4
        if mats == 1:
            outs += (sds((block_rows, hidden_width), bf16),)
            out_specs += (vmem_space,)
        return call(
            kernel,
            outs,
            (products, got, *olds, first_moment[0], second_moment[0], *previous),
            [smem_space] + [vmem_space] * (1 + mats) + [block] * 2 + [any_space] * len(previous),
            out_specs=out_specs,
            aliases={4 + mats + i: i for i in range(len(previous))},
            grid=(1,),
            name="update",
            vmem=4 * got.shape[0] * got.shape[1] * 256 + 10 * mebi,
        )

    *partial_out, new_down = update(1, 2, masters[2:], ())
    downs = [new_down[None]]
    for bit in range(outer_bits):
        downs = [jnp.concatenate(downs)] if len(downs) > 1 else downs
        downs = [downs[0], swapped(downs[0], "dp", inner_bits + bit)]
    slot_outputs = call(
        functools.partial(project_kernel, group),
        sds((group, experts, pool, outer * block_rows), bf16),
        (my_ids, *hidden_parts, *downs),
        [smem_space] + [vmem_space] * (group + len(downs)),
        scratch=(
            pltpu.VMEM((hidden_width, total), bf16),
            pltpu.VMEM((outer * block_rows, hidden_width), bf16),
        ),
        name="project",
        vmem=12 * total * outer * block_rows + 12 * mebi,
    )
    slot_outputs = slot_outputs.reshape(group * experts, pool, outer * block_rows)
    columns = lax.all_to_all(
        slot_outputs, ("dp", "expert"), 0, 0, axis_index_groups=cubes, tiled=True
    )
    outs = update(2, 0, masters[:2], partial_out)
    forward = call(
        functools.partial(finish_kernel, experts, block_rows),
        sds((pool, width), bf16),
        (columns,),
        [vmem_space],
        name="finish",
    )
    return (*[out[None] for out in outs], forward)


def solution(mesh):
    in_specs = (
        P(("dp", "expert"), None),
        P(("dp", "expert"), None),
        P(("dp", "expert")),
        P(("dp", "expert"), None),
        P("expert", "dp", None),
        P("expert", "dp", None),
        P("expert", "dp", None),
        P("expert", None, "dp", None),
        P("expert", None, "dp", None),
    )
    out_specs = (
        P("expert", None, "dp", None),
        P("expert", None, "dp", None),
        P("expert", None, "dp", None),
        P("expert", None, "dp", None),
        P(("dp", "expert"), None),
    )
    return jax.shard_map(shards, mesh=mesh, in_specs=in_specs, out_specs=out_specs, check_vma=False)
```

```python
import functools

import jax
import jax.numpy as jnp
from jax import lax
from jax.experimental import pallas as pl
from jax.experimental.pallas import tpu as pltpu
from jax.sharding import PartitionSpec as P

first_decay = 0.9
second_decay = 0.95
learn_rate = 0.01
adam_eps = 1e-08
weight_decay = 0.1
adam_count = 100.0
norm_eps = 1e-06
gathered_limit = 16
mask_lanes = 128
mebi = 1024 * 1024
vmem_bytes = 14 * mebi
vmem_most = 56 * mebi
f32 = jnp.float32
bf16 = jnp.bfloat16
any_space = pl.BlockSpec(memory_space=pl.ANY)
smem_space = pl.BlockSpec(memory_space=pltpu.SMEM)
vmem_space = pl.BlockSpec(memory_space=pltpu.VMEM)


def swapped(array, axis, bit):
    return lax.ppermute(array, axis, [(i, i ^ 1 << bit) for i in range(lax.axis_size(axis))])


def bits_of(size):
    return size.bit_length() - 1


def cube_gather(array, steps):
    pieces = {(0, 0): array}
    for axis, bit in steps:
        for (e, k), piece in list(pieces.items()):
            key = (e ^ (1 << bit), k) if axis == "expert" else (e, k ^ (1 << bit))
            pieces[key] = swapped(piece, axis, bit)
    return pieces


def waved_gather(mine, x_rows, sent, exchange, ids):
    z = lambda value: swapped(value, "dp", 2)
    y = lambda value: swapped(value, "dp", 1)
    x = lambda value: swapped(value, "expert", 0)
    from_z, from_y, from_x = z(mine), y(mine), x(mine)
    weights = exchange(sent)
    from_z, from_y, from_x, weights = lax.optimization_barrier((from_z, from_y, from_x, weights))
    from_zy, from_zx = y(from_z), x(from_z)
    from_zyx = [x(from_zy[:x_rows]), y(from_zx[x_rows:])]
    from_y, from_x, from_zy, from_zx = lax.optimization_barrier((from_y, from_x, from_zy, from_zx))
    from_yx = [x(from_y[:x_rows]), y(from_x[x_rows:])]
    from_z, from_y, from_x, mine, ids, *_ = lax.optimization_barrier(
        (from_z, from_y, from_x, mine, ids, from_zy, from_zx)
    )
    pieces = {
        (0, 0): [mine],
        (0, 4): [from_z],
        (0, 2): [from_y],
        (1, 0): [from_x],
        (0, 6): [from_zy],
        (1, 4): [from_zx],
        (1, 2): from_yx,
        (1, 6): from_zyx,
    }
    for (e, k), held in list(pieces.items()):
        pieces[e, k | 1] = [swapped(piece, "dp", 0) for piece in held]
    return pieces, weights, ids


def tree_sum(value, bits):
    for bit in bits:
        value = value + swapped(value, "dp", bit)
    return value


def nt(a, b):
    return lax.dot_general(a, b, (((1,), (1,)), ((), ())), preferred_element_type=f32)


def tn(a, b):
    return lax.dot_general(a, b, (((0,), (0,)), ((), ())), preferred_element_type=f32)


def tree_weights(entry, count):
    gram = {(i, j): entry(i, j) for i in range(count) for j in range(i, count)}
    weights = [None] * count
    size = count
    while size > 1:
        scale = []
        for j in range(0, size, 2):
            cross = gram[j, j + 1]
            scale.append(1.0 - cross / (2.0 * (gram[j, j] + norm_eps)))
            scale.append(1.0 - cross / (2.0 * (gram[j + 1, j + 1] + norm_eps)))
        span = count // size
        for leaf in range(count):
            factor = scale[leaf // span]
            weights[leaf] = factor if weights[leaf] is None else weights[leaf] * factor
        full = lambda i, j: gram[min(i, j), max(i, j)] * (scale[i] * scale[j])
        size //= 2
        if size > 1:
            gram = {
                (i, j): full(2 * i, 2 * j)
                + full(2 * i, 2 * j + 1)
                + full(2 * i + 1, 2 * j)
                + full(2 * i + 1, 2 * j + 1)
                for i in range(size)
                for j in range(i, size)
            }
    return weights


def prepare_kernel(
    route_ref, counts_ref, tok_ref, cot_ref, gate_ref, up_ref, down_ref, out_ref, sent_ref
):
    group, part = sent_ref.shape[0], sent_ref.shape[1] // 3
    for index, ref in enumerate((gate_ref, up_ref, down_ref)):
        turned = ref[...].T.astype(bf16)
        for k in range(group):
            sent_ref[k, index * part : (index + 1) * part, :] = turned[k * part : (k + 1) * part, :]
    pool, width = cot_ref.shape
    experts, capacity = route_ref.shape
    out_ref[:pool, :width] = tok_ref[...]
    out_ref[:pool, width:] = jnp.zeros((pool, mask_lanes), bf16)
    out_ref[pool:, :width] = cot_ref[...]
    ids = lax.broadcasted_iota(jnp.int32, (pool, capacity), 0)
    slots = lax.broadcasted_iota(jnp.int32, (pool, capacity), 1)
    lanes = lax.broadcasted_iota(jnp.int32, (pool, mask_lanes), 1)
    flags = jnp.zeros((pool, mask_lanes), f32)
    for e in range(experts):
        named = (ids == route_ref[e : e + 1, :]) & (slots < counts_ref[0, e])
        found = jnp.sum(named.astype(f32), axis=1, keepdims=True)
        flags = jnp.where(lanes == e, found, flags)
    out_ref[pool:, width:] = flags.astype(bf16)


def place_rows(layout, refs, into, first, lanes, rows, pool, members):
    for (e, k), held in layout.items():
        low, at = 0, k * rows + e * pool
        for index, count in held:
            begin, end = max(low, first), min(low + count, first + pool)
            if begin < end and k in members:
                source = refs[index][begin - low : end - low, :lanes]
                into[at + begin - first : at + end - first, :] = source
            low += count


def gather_kernel(layout, experts, group, pool, pieces, idx_ref, *refs):
    shared, held, refs = refs[:pieces], refs[pieces:-9], refs[-9:]
    hid_ref, hid_abs_ref, dgate_ref, dup_ref, gram_ref, x_ref, y_ref, w_ref, row_ref = refs
    slot, expert, outer_index = idx_ref[0], idx_ref[1], idx_ref[2]
    part, total = hid_ref.shape
    rows = total // group
    width = x_ref.shape[1]
    per, _, _, block_rows = held[0].shape
    for o in range(per * len(held)):
        for h, ref in enumerate(held):

            @pl.when(((outer_index ^ o) // per) == h)
            def _(ref=ref, o=o):
                source = ref.at[(outer_index ^ o) % per]
                for b in range(group):
                    at = (o * group + b) * block_rows
                    w_ref[:, at : at + block_rows] = source[b]

    row_ref[...] = jnp.zeros_like(row_ref)
    pick = lax.broadcasted_iota(jnp.int32, (8, mask_lanes), 1) == expert
    both_members = max(1, min(group, 256 // rows))
    for first in range(0, group, both_members):
        members = range(first, first + both_members)
        mine, end = slice(first * rows, (first + both_members) * rows), (first + both_members) * rows
        place_rows(layout, shared, x_ref, 0, width, rows, pool, members)
        place_rows(layout, shared, y_ref, pool, width + mask_lanes, rows, pool, members)
        pre = nt(w_ref[: 2 * part, :], x_ref[mine, :])
        outer_x = nt(x_ref[mine, :], x_ref[:end, :])
        back_hidden = nt(w_ref[2 * part :, :], y_ref[mine, :width])
        outer_y = nt(y_ref[mine, :width], y_ref[:end, :width])
        mask = nt(pick.astype(bf16), y_ref[mine, width:])[0:1] > 0.5
        gate_pre, up_pre = pre[:part], pre[part:]
        sigmoid_gate = jax.nn.sigmoid(gate_pre)
        active_gate = gate_pre * sigmoid_gate
        kept = lambda value: jnp.where(mask, value, 0.0).astype(bf16)
        hidden = kept(active_gate * up_pre)
        hid_ref[:, mine] = hidden
        for n, k in enumerate(members):
            at = pl.multiple_of((slot ^ k) * rows, rows)
            hid_abs_ref[:, pl.ds(at, rows)] = hidden[:, n * rows : (n + 1) * rows]
        dgate_ref[:, mine] = kept(
            back_hidden * up_pre * sigmoid_gate * (1.0 + gate_pre * (1.0 - sigmoid_gate))
        )
        dup_ref[:, mine] = kept(back_hidden * active_gate)
        for m, (ref, prod) in enumerate(
            ((dgate_ref, outer_x), (dup_ref, outer_x), (hid_ref, outer_y))
        ):
            both = prod * tn(ref[:, mine], ref[:, :end])
            for n, k in enumerate(members):
                sums = both[n * rows : (n + 1) * rows, : (k + 1) * rows].sum(0, keepdims=True)
                row_ref[m * group + k : m * group + k + 1, : (k + 1) * rows] = sums
    lanes = lax.broadcasted_iota(jnp.int32, gram_ref.shape, 1)
    relative = jnp.zeros(gram_ref.shape, f32)
    for k in range(group):
        sums = row_ref[:, k * rows : (k + 1) * rows].sum(1, keepdims=True)
        relative = jnp.where(lanes == (slot ^ k), sums, relative)
    row_ids = lax.broadcasted_iota(jnp.int32, gram_ref.shape, 0)
    gram = jnp.zeros(gram_ref.shape, f32)
    for m in range(3):
        for k in range(group):
            row = relative[m * group + k : m * group + k + 1]
            gram = jnp.where(row_ids == m * group + (slot ^ k), row, gram)
    gram_ref[...] = gram


def vector_kernel(group, idx_ref, gram_ref, x_ref, y_ref, dgate_ref, dup_ref, hid_ref, out_ref):
    part, total = hid_ref.shape
    rows = total // group
    count, _, block_rows = out_ref.shape
    width = count * block_rows
    slot = idx_ref[0]

    def scaled(m, ref):
        def entry(i, j):
            a, b = slot ^ i, slot ^ j
            value = gram_ref[m * group + a, b]
            if i != j:
                value = value + gram_ref[m * group + b, a]
            return jnp.full((1, rows), value, f32)

        weights = tree_weights(entry, group)
        return jnp.concatenate(
            [
                (ref[:, d * rows : (d + 1) * rows].astype(f32) * weights[d]).astype(bf16)
                for d in range(group)
            ],
            axis=1,
        )

    pair = jnp.concatenate([scaled(0, dgate_ref), scaled(1, dup_ref)], axis=0)
    vectors = (
        jnp.dot(pair, x_ref[:, :width], preferred_element_type=f32).astype(bf16),
        jnp.dot(scaled(2, hid_ref), y_ref[:, :width], preferred_element_type=f32).astype(bf16),
    )
    for i in range(count):
        lanes = slice(i * block_rows, (i + 1) * block_rows)
        out_ref[i, : 2 * part, :] = vectors[0][:, lanes]
        out_ref[i, 2 * part :, :] = vectors[1][:, lanes]


def update_kernel(group, mats, start, gram_ref, got_ref, *refs):
    masters = refs[:mats]
    first_ref, second_ref = refs[mats : mats + 2]
    outs = refs[-5:] if mats == 1 else refs[-4:]
    sum_ref, new_ref, new_first_ref, new_second_ref = outs[:4]
    outer = got_ref.shape[0] // group
    block_rows = got_ref.shape[2]
    part = got_ref.shape[1] // 3
    for m in range(mats):
        n = start + m
        entry = lambda i, j: jnp.full((1, block_rows), gram_ref[n * outer + i, j], f32)
        weights = tree_weights(entry, outer)
        total = 0.0
        for o in range(outer):
            held = [
                got_ref[o * group + s, n * part : (n + 1) * part, :].astype(f32)
                for s in range(group)
            ]
            total = total + weights[o] * jnp.concatenate(held, axis=0)
        total = total.T
        first = first_decay * first_ref[m] + (1.0 - first_decay) * total
        second = second_decay * second_ref[m] + (1.0 - second_decay) * total * total
        first_hat = first / (1.0 - first_decay**adam_count)
        second_hat = second / (1.0 - second_decay**adam_count)
        old = masters[m][...]
        new = old - learn_rate * (first_hat / (jnp.sqrt(second_hat) + adam_eps) + weight_decay * old)
        sum_ref[m] = total
        new_ref[m] = new
        new_first_ref[m] = first
        new_second_ref[m] = second
        if mats == 1:
            outs[-1][...] = new.astype(bf16)


def project_kernel(group, idx_ref, *refs):
    parts, downs, (out_ref, hidden_ref, all_ref) = refs[:group], refs[group:-3], refs[-3:]
    slot, expert, outer_index = idx_ref[0], idx_ref[1], idx_ref[2]
    bits, part = bits_of(group), parts[0].shape[0]
    for n, ref in enumerate(parts):
        relative = sum((n >> b & 1) << (bits - 1 - b) for b in range(bits))
        at = pl.multiple_of((slot ^ relative) * part, 16)
        hidden_ref[pl.ds(at, part), :] = ref[...]
    per, block_rows = downs[0].shape[:2]
    for o in range(per * len(downs)):
        for h, ref in enumerate(downs):

            @pl.when(((outer_index ^ o) // per) == h)
            def _(ref=ref, o=o):
                all_ref[o * block_rows : (o + 1) * block_rows, :] = ref[(outer_index ^ o) % per]

    made = lax.dot_general(
        hidden_ref[...], all_ref[...], (((0,), (1,)), ((), ())), preferred_element_type=f32
    )
    experts, pool = out_ref.shape[1], out_ref.shape[2]
    for d in range(out_ref.shape[0]):
        for e in range(experts):
            at = (d * experts + e) * pool
            out_ref[d, expert ^ e] = made[at : at + pool].astype(bf16)


def finish_kernel(experts, block_rows, got_ref, out_ref):
    group = got_ref.shape[0] // experts
    for o in range(got_ref.shape[2] // block_rows):
        for s in range(group):
            lanes = slice(o * block_rows, (o + 1) * block_rows)
            total = got_ref[s * experts, :, lanes].astype(f32)
            for e in range(1, experts):
                total = total + got_ref[s * experts + e, :, lanes].astype(f32)
            at = (o * group + s) * block_rows
            out_ref[:, at : at + block_rows] = total.astype(bf16)


def call(kernel, outs, args, in_specs, scratch=(), out_specs=None, aliases=None, name=None, grid=(), vmem=vmem_bytes):
    return pl.pallas_call(
        kernel,
        out_shape=outs,
        grid=grid,
        in_specs=in_specs,
        out_specs=out_specs if out_specs is not None else jax.tree.map(lambda _: vmem_space, outs),
        scratch_shapes=list(scratch),
        compiler_params=pltpu.CompilerParams(vmem_limit_bytes=min(vmem, vmem_most)),
        input_output_aliases=aliases or {},
        name=name,
    )(*args)


def after(value, *others):
    return lax.optimization_barrier((value, *others))[0]


def shards(
    tokens,
    cotangent,
    route,
    counts,
    gate_master,
    up_master,
    down_master,
    first_moment,
    second_moment,
):
    experts = lax.axis_size("expert")
    dp = lax.axis_size("dp")
    group = max(1, min(gathered_limit // experts, dp))
    inner_bits = bits_of(group)
    outer_bits = bits_of(dp // group)
    outer = dp // group
    dp_bits = inner_bits + outer_bits
    pool, width = tokens.shape
    rows = experts * pool
    total = group * rows
    block_rows, hidden_width = gate_master.shape[1:]
    part = hidden_width // group
    my_dp = lax.axis_index("dp")
    expert_index = lax.axis_index("expert")
    my_ids = jnp.stack([my_dp % group, expert_index, my_dp // group]).astype(jnp.int32)
    groups = [[o * group + s for s in range(group)] for o in range(outer)]
    cubes = [[o * group * experts + s for s in range(group * experts)] for o in range(outer)]
    capacity = route.shape[0] // experts
    sds = jax.ShapeDtypeStruct
    masters = [gate_master[0], up_master[0], down_master[0]]

    mine, sent = call(
        prepare_kernel,
        (
            sds((2 * pool, width + mask_lanes), bf16),
            sds((group, 3 * part, block_rows), bf16),
        ),
        (route.reshape(experts, capacity), counts, tokens, cotangent, *masters),
        [vmem_space, smem_space] + [vmem_space] * 5,
        name="prepare",
        vmem=vmem_most,
    )
    exchange = lambda sent: lax.all_to_all(
        sent, "dp", 0, 0, axis_index_groups=groups, tiled=True
    )
    if inner_bits == 3 and experts == 2:
        pieces, own_group, my_ids = waved_gather(
            mine, -(-4 * pool // 64) * 16, sent, exchange, my_ids
        )
    else:
        steps = [("expert", b) for b in range(bits_of(experts))]
        steps += [("dp", b) for b in reversed(range(inner_bits))]
        pieces = {key: [value] for key, value in cube_gather(mine, steps).items()}
        own_group = exchange(sent)
    shared, layout = [], {}
    for key, parts in pieces.items():
        layout[key] = [(len(shared) + n, piece.shape[0]) for n, piece in enumerate(parts)]
        shared += parts
    held = [own_group[None]]
    for bit in range(outer_bits):
        held = [jnp.concatenate(held)] if len(held) > 1 else held
        held = [held[0], swapped(held[0], "dp", inner_bits + bit)]
    wide = width + mask_lanes
    factor = sds((part, total), bf16)
    gram_rows = -(-3 * group // 8) * 8
    rows_bytes, weight_bytes = 4 * total * wide, 6 * part * width
    hidden, hidden_own, d_gate, d_up, gram, token_all, grad_all = call(
        functools.partial(gather_kernel, layout, experts, group, pool, len(shared)),
        (
            *(factor,) * 4,
            sds((gram_rows, 128), f32),
            sds((total, width), bf16),
            sds((total, wide), bf16),
        ),
        (my_ids, *shared, *held),
        [smem_space] + [vmem_space] * (len(shared) + len(held)),
        scratch=(
            pltpu.VMEM((3 * part, width), bf16),
            pltpu.VMEM((gram_rows, total), f32),
        ),
        name="forward_and_gram",
        vmem=5 * rows_bytes // 2 + 3 * weight_bytes + 4 * total * total * (outer // 4),
    )
    gram = tree_sum(gram, range(inner_bits - 1))
    hidden_parts = [hidden_own]
    for bit in reversed(range(1, inner_bits)):
        hidden_parts += [swapped(piece, "dp", bit) for piece in hidden_parts]
    gram = tree_sum(gram, range(inner_bits - 1, inner_bits))

    vector = call(
        functools.partial(vector_kernel, group),
        sds((dp, 3 * part, block_rows), bf16),
        (my_ids, gram, token_all, grad_all, d_gate, d_up, hidden),
        [smem_space] * 2 + [vmem_space] * 5,
        name="local_tree",
        vmem=5 * rows_bytes // 4 + 2 * weight_bytes + 8 * mebi,
    )
    got = lax.all_to_all(after(vector, *hidden_parts[1:2]), "dp", 0, 0, tiled=True)
    hidden_parts += [swapped(piece, "dp", 0) for piece in hidden_parts]
    leaves = got.reshape(outer, group, 3, part, block_rows).transpose(2, 0, 1, 3, 4)
    leaves = leaves.reshape(3, outer, hidden_width, block_rows).astype(f32)
    if outer > 2:
        products = jnp.einsum("miab,mjab->mij", leaves, leaves, precision=lax.Precision.HIGHEST)
    else:
        products = (leaves[:, :, None] * leaves[:, None]).sum((3, 4))
    products = tree_sum(products.reshape(3 * outer, outer), range(dp_bits))

    def update(mats, start, olds, previous):
        place = lambda i: (start // mats, 0, 0)
        block = pl.BlockSpec((mats, block_rows, hidden_width), place)
        whole = sds((3, block_rows, hidden_width), f32)
        kernel = functools.partial(update_kernel, group, mats, start)
        outs, out_specs = (whole,) * 4, (block,) * 4
        if mats == 1:
            outs += (sds((block_rows, hidden_width), bf16),)
            out_specs += (vmem_space,)
        return call(
            kernel,
            outs,
            (products, got, *olds, first_moment[0], second_moment[0], *previous),
            [smem_space] + [vmem_space] * (1 + mats) + [block] * 2 + [any_space] * len(previous),
            out_specs=out_specs,
            aliases={4 + mats + i: i for i in range(len(previous))},
            grid=(1,),
            name="update",
            vmem=4 * got.shape[0] * got.shape[1] * 256 + 10 * mebi,
        )

    *partial_out, new_down = update(1, 2, masters[2:], ())
    downs = [new_down[None]]
    for bit in range(outer_bits):
        downs = [jnp.concatenate(downs)] if len(downs) > 1 else downs
        downs = [downs[0], swapped(downs[0], "dp", inner_bits + bit)]
    slot_outputs = call(
        functools.partial(project_kernel, group),
        sds((group, experts, pool, outer * block_rows), bf16),
        (my_ids, *hidden_parts, *downs),
        [smem_space] + [vmem_space] * (group + len(downs)),
        scratch=(
            pltpu.VMEM((hidden_width, total), bf16),
            pltpu.VMEM((outer * block_rows, hidden_width), bf16),
        ),
        name="project",
        vmem=12 * total * outer * block_rows + 12 * mebi,
    )
    slot_outputs = slot_outputs.reshape(group * experts, pool, outer * block_rows)
    columns = lax.all_to_all(
        slot_outputs, ("dp", "expert"), 0, 0, axis_index_groups=cubes, tiled=True
    )
    outs = update(2, 0, masters[:2], partial_out)
    forward = call(
        functools.partial(finish_kernel, experts, block_rows),
        sds((pool, width), bf16),
        (columns,),
        [vmem_space],
        name="finish",
    )
    return (*[out[None] for out in outs], forward)


def solution(mesh):
    in_specs = (
        P(("dp", "expert"), None),
        P(("dp", "expert"), None),
        P(("dp", "expert")),
        P(("dp", "expert"), None),
        P("expert", "dp", None),
        P("expert", "dp", None),
        P("expert", "dp", None),
        P("expert", None, "dp", None),
        P("expert", None, "dp", None),
    )
    out_specs = (
        P("expert", None, "dp", None),
        P("expert", None, "dp", None),
        P("expert", None, "dp", None),
        P("expert", None, "dp", None),
        P(("dp", "expert"), None),
    )
    return jax.shard_map(shards, mesh=mesh, in_specs=in_specs, out_specs=out_specs, check_vma=False)
```
